256 devices in a mesh: outer: 16 (over y, x_hi, core), inner: 16 (over x_lo, z).
Axes of the slice: x: 4 (x_hi: 2, x_lo: 2; x = x_hi * 2 + x_lo), y: 4, z: 8, core: 2. Of those that a mesh axis runs over, the one named last changes fastest.
Arguments:
- residual_in: bfloat16 [65536, 3200], P(('outer', 'inner')), may hold values from -6 to 6
- queries: bfloat16 [65536, 1664], P(('outer', 'inner')), may hold values from -80 to 80
- keys: bfloat16 [65536, 1664], P(('outer', 'inner')), may hold values from -4.5 to 4.5
- values: bfloat16 [65536, 1664], P(('outer', 'inner')), may hold values from -12 to 12
- segment_ids: int32 [256, 256], P(('outer', 'inner')), may hold values from 0 to 7, never falling along the last dimension, each value on 1 to 128 neighbouring positions
- weight_codes: bfloat16 [3200, 1664], P('inner'), may hold values from -15 to 15, as said below
- weight_exponents: int32 [3200, 52], P('inner'), may hold values from -10 to -7
- out_grad: bfloat16 [65536, 3200], P(('outer', 'inner')), may hold values from -24 to 24
Outputs:
- layer_out: bfloat16 [65536, 3200], P(('outer', 'inner'))
- query_grad: bfloat16 [65536, 1664], P(('outer', 'inner'))
- key_grad: bfloat16 [65536, 1664], P(('outer', 'inner'))
- value_grad: bfloat16 [65536, 1664], P(('outer', 'inner'))
- weight_grad: float32 [3200, 1664], P('inner', 'outer')
The draws below stay inside these ranges and needn't reach their ends.
Inputs may be any that keep to these rules, and one draw needn't show every extreme that they name: `weight_codes`: signed codes with four significant bits, magnitudes from 1/4 to 15.
All inputs are finite; a program needn't handle non-finite values.
Results may differ from the reference program's by a relative error of at most 0.025.
Values may be sent and summed in bfloat16 or wider, within the bound.
A program may use at most 128 MiB of HBM per device.

```python
import math
import jax
import jax.numpy as jnp
import numpy as np
from jax import lax

D = 3200
HEADS = 13
BLOCK = 32
TOK_DEV = 256
HD = 1664
IMAGES = 8
TOKENS = 65536
DEVICES = 256


def key_base(key):
    return jax.random.truncated_normal(key, -4.0, 4.0, (TOKENS, HD), jnp.float32)


def draw_keys(key, part):
    base = key_base(key)
    return base.astype(jnp.bfloat16)


def draw_queries(key, part):
    key = jax.random.fold_in(key, 7)
    fresh = jax.random.truncated_normal(key, -4.0, 4.0, (TOKENS, HD), jnp.float32)
    return fresh.astype(jnp.bfloat16)


def draw_weight_codes(key, part):
    key = jax.random.fold_in(key, 5)
    first, second, third = jax.random.split(key, 3)
    mantissa = jax.random.randint(first, (D, HD), 0, 8).astype(jnp.float32)
    octave = jax.random.randint(second, (D, HD), -2, 4)
    signs = (jax.random.randint(third, (D, HD), 0, 2) * 2 - 1).astype(jnp.float32)
    twos = jnp.zeros((D, HD), jnp.float32)
    for power in range(-2, 4):
        twos = twos + jnp.where(octave == power, 2.0 ** power, 0.0)
    return (signs * (1.0 + mantissa / 8.0) * twos).astype(jnp.bfloat16)


def plant(values, key, least, top_value):
    place = [jax.random.randint(jax.random.fold_in(key, axis), (), 0, length) for axis, length in enumerate(values.shape)]
    longest = values.shape.index(max(values.shape))
    next_to = place[:longest] + [(place[longest] + 1) % values.shape[longest]] + place[longest + 1:]
    return values.at[tuple(place)].set(least).at[tuple(next_to)].set(top_value)


def raised(result, key, source, target, blocks, factor):
    owner, partner = [(jnp.arange(result.shape[dim]) // (result.shape[dim] // blocks)).reshape([-1 if axis == dim else 1 for axis in range(result.ndim)]) for dim in (source, target)]
    chosen = jax.random.permutation(key, blocks)[partner]
    strong = (owner == chosen) | (owner == (partner + blocks // 2) % blocks)
    return jnp.where(strong, factor * result, result)


def levels(own_key, dims, cuts, low, largest):
    def one(position, parts):
        steps = jax.random.uniform(jax.random.fold_in(jax.random.fold_in(own_key, 6), position), (parts,), jnp.float32, low / len(cuts), largest / len(cuts))
        return jnp.repeat(jnp.exp(steps), dims[position] // parts).reshape((-1,) + (1,) * (len(dims) - position - 1))

    factor_of = one(*cuts[0])
    for cut in cuts[1:]:
        factor_of = factor_of * one(*cut)
    return factor_of


def length_profile(number_of, total, most, slope):
    weights = [(1 << 20) // math.isqrt(grade ** slope) + 1 for grade in range(2, number_of + 1)]
    surplus, holding = total - most - (number_of - 1), [1] * (number_of - 1)
    while surplus > 0:
        candidates = [i for i in range(number_of - 1) if holding[i] < most]
        mass, budget = sum([weights[i] for i in candidates]), surplus
        for i in candidates:
            more = min(most - holding[i], max(1, budget * weights[i] // mass), surplus)
            holding[i] = holding[i] + more
            surplus = surplus - more
    return np.array([most] + holding)


def ragged_sizes(own_key, count, total, reach, slope):
    if count == 2:
        one = jax.random.randint(own_key, (), max(1, total - reach), min(reach, total - 1) + 1)
        return jnp.stack([one, total - one])
    lengths = jnp.asarray(length_profile(count, total, reach, slope), jnp.int32)
    couples = (count - 1) // 2
    giver, receiver = lengths[1:1 + 2 * couples:2], lengths[2:2 + 2 * couples:2]
    slack = jnp.minimum(giver - 1, reach - receiver)
    passed = jax.random.randint(jax.random.fold_in(own_key, 1), (couples,), 0, 1 << 20) % (slack + 1)
    lengths = lengths.at[1:1 + 2 * couples:2].set(giver - passed).at[2:2 + 2 * couples:2].set(receiver + passed)
    return lengths[jax.random.permutation(jax.random.fold_in(own_key, 2), count)]


def centred(rng, shape, deviation, most, cuts=(), dtype=jnp.bfloat16):
    gain = levels(rng, shape, cuts, -0.22, 0.18) if cuts else 1.0
    result = jax.random.normal(rng, shape, jnp.float32) * deviation * gain
    return jnp.minimum(jnp.maximum(result, -most), most).astype(dtype)


def bell_draw_with(own_key, shape, spread, reach, pieces, heavy, held_as=jnp.bfloat16):
    result = spread * jax.random.normal(own_key, shape, jnp.float32)
    if pieces:
        result = result * levels(own_key, shape, pieces, -0.22, 0.18)
    return jnp.clip(raised(result, jax.random.fold_in(own_key, 3), *heavy), -reach, reach).astype(held_as)


def setup_inputs(seed: int = 0) -> dict:
    seeds = jax.random.split(jax.random.key(seed), 9)
    residual_in = centred(seeds[0], (TOKENS, D), 1.0, 6.0, ((0, 256),))
    queries = draw_queries(jax.random.fold_in(seeds[8], 71), 0)
    keys = draw_keys(jax.random.fold_in(seeds[8], 71), 0)
    values = centred(seeds[3], (TOKENS, HD), 3.0, 12.0, ((0, 256),))
    segment_ids = jax.vmap(lambda own: jnp.searchsorted(jnp.cumsum(ragged_sizes(own, IMAGES, TOK_DEV, TOK_DEV // 2, 2)), jnp.arange(TOK_DEV), side="right"))(jax.random.split(seeds[4], DEVICES)).reshape((DEVICES, TOK_DEV)).astype(jnp.int32)
    weight_codes = draw_weight_codes(jax.random.fold_in(seeds[8], 71), 0)
    weight_exponents = plant(jax.random.randint(seeds[6], (D, HD // BLOCK), -10, -6), jax.random.fold_in(seeds[6], 1), -10, (-6) - 1).astype(jnp.int32)
    out_grad = bell_draw_with(seeds[7], (TOKENS, D), 1.0, 24.0, ((0, 256),), (0, 1, 128, 5.5))
    return {"residual_in": residual_in, "queries": queries, "keys": keys, "values": values, "segment_ids": segment_ids, "weight_codes": weight_codes, "weight_exponents": weight_exponents, "out_grad": out_grad}


def power_of_two(exponents):
    total = jnp.zeros(exponents.shape, jnp.float32)
    for octave in range(-16, 1):
        total = total + jnp.where(exponents == octave, 2.0 ** octave, 0.0)
    return total

def dequantize(codes, exponents):
    scales = jnp.repeat(power_of_two(exponents), codes.shape[1] // exponents.shape[1], axis=1)
    return (codes.astype(jnp.float32) * scales).astype(jnp.bfloat16)

def heads_first(array):
    return array.reshape(array.shape[0], HEADS, array.shape[1] // HEADS).transpose(1, 0, 2)

def heads_last(array):
    return array.transpose(1, 0, 2).reshape(array.shape[1], array.shape[0] * array.shape[2])

def head_probs(query, key_rows, same):
    scores = lax.dot_general(query, key_rows, (((1,), (1,)), ((), ())), preferred_element_type=jnp.float32)
    scores = scores * (1.0 / math.sqrt(query.shape[1]))
    return jax.nn.softmax(jnp.where(same, scores, -jnp.inf), axis=-1)

def pack_forward(queries, keys, values, segments):
    same = segments[:, None] == segments[None, :]

    def one_head(triple):
        query, key_rows, value_rows = triple
        rounded = head_probs(query, key_rows, same).astype(jnp.bfloat16)
        return jnp.dot(rounded, value_rows, preferred_element_type=jnp.float32).astype(jnp.bfloat16)
    return heads_last(lax.map(one_head, (heads_first(queries), heads_first(keys), heads_first(values))))

def pack_backward(queries, keys, values, segments, attended, attended_grad):
    same = segments[:, None] == segments[None, :]

    def one_head(group):
        query, key_rows, value_rows, output, output_grad = group
        probs = head_probs(query, key_rows, same)
        rounded = probs.astype(jnp.bfloat16)
        value_grad = lax.dot_general(rounded, output_grad, (((0,), (0,)), ((), ())), preferred_element_type=jnp.float32).astype(jnp.bfloat16)
        prob_grad = lax.dot_general(output_grad, value_rows, (((1,), (1,)), ((), ())), preferred_element_type=jnp.float32)
        delta = lax.optimization_barrier(jnp.sum(output_grad.astype(jnp.float32) * output.astype(jnp.float32), axis=1, keepdims=True))
        score_grad = (probs * (prob_grad - delta)).astype(jnp.bfloat16)
        factor = 1.0 / math.sqrt(query.shape[1])
        query_grad = (jnp.dot(score_grad, key_rows, preferred_element_type=jnp.float32) * factor).astype(jnp.bfloat16)
        key_grad = (lax.dot_general(score_grad, query, (((0,), (0,)), ((), ())), preferred_element_type=jnp.float32) * factor).astype(jnp.bfloat16)
        return (query_grad, key_grad, value_grad)
    stacked = lax.map(one_head, (heads_first(queries), heads_first(keys), heads_first(values), heads_first(attended), heads_first(attended_grad)))
    return tuple((heads_last(member) for member in stacked))

def reference(residual_in, queries, keys, values, segment_ids, weight_codes, weight_exponents, out_grad):
    weight = dequantize(weight_codes, weight_exponents)

    def by_pack(array):
        return array.reshape(DEVICES, TOK_DEV, array.shape[1])
    attended = lax.map(lambda group: pack_forward(*group), (by_pack(queries), by_pack(keys), by_pack(values), segment_ids))
    attended = attended.reshape(TOKENS, HD)
    projected = lax.dot_general(attended, weight, (((1,), (1,)), ((), ())), preferred_element_type=jnp.float32)
    layer_out = (residual_in.astype(jnp.float32) + projected).astype(jnp.bfloat16)
    attended_grad = jnp.dot(out_grad, weight, preferred_element_type=jnp.float32).astype(jnp.bfloat16)

    def add_partial(total, group):
        grad_rows, attended_rows = group
        partial_sum = lax.dot_general(grad_rows, attended_rows, (((0,), (0,)), ((), ())), preferred_element_type=jnp.float32).astype(jnp.bfloat16)
        partial_sum = lax.optimization_barrier(partial_sum)
        return (total + partial_sum.astype(jnp.float32), None)
    total, unused = lax.scan(add_partial, jnp.zeros((D, HD), jnp.float32), (by_pack(out_grad), by_pack(attended)))
    weight_grad = total * (1.0 / math.sqrt(TOKENS))
    stacked = lax.map(lambda group: pack_backward(*group), (by_pack(queries), by_pack(keys), by_pack(values), segment_ids, by_pack(attended), by_pack(attended_grad)))
    query_grad = stacked[0].reshape(TOKENS, HD)
    key_grad = stacked[1].reshape(TOKENS, HD)
    value_grad = stacked[2].reshape(TOKENS, HD)
    return (layer_out, query_grad, key_grad, value_grad, weight_grad)
```

```python
import functools
import math

import jax
import jax.numpy as jnp
from jax import lax
from jax.experimental import pallas as pl
from jax.experimental.pallas import tpu as pltpu
from jax.sharding import PartitionSpec as P

MESH = pl.DeviceIdType.MESH
BF = jnp.bfloat16
F32 = jnp.float32

TOK = 256
D = 3200
HD = 1664
HEADS = 13
BLOCK = 32
T = 128
RB = 200
RP = 208
SPAN = ((0, 112), (112, 96))
CARRY = 1152
SHARE = 512
TOP = (4, 3)


def chain(way, half):
    return TOP[half] if way == 0 else TOP[1 - half]


def dot(a, b, ca, cb):
    return lax.dot_general(a, b, (((ca,), (cb,)), ((), ())), preferred_element_type=F32)


def lanes(rows):
    return lax.broadcasted_iota(jnp.int32, (rows, T), 1)


def body_kernel(
    seg_ref, codes_ref, exps_ref, q_hbm, k_hbm, v_hbm, og_hbm, res_hbm,
    lo_hbm, dq_hbm, dk_hbm, dv_hbm, wg_ref,
    W, PG, YR, XR, ZR, LB, FR, SR, SS, OGR, OGS, ATR, ATT, PST, AGF, AGB, Q, K, V, OG, LO, BIAS,
    in_sem, out_sem, zs, zr, xs, xr, ys, yr, ss, sr, gys, gyr, gxs, gxr, gzs, gzr, fs, fr, cs, cr,
):
    o = lax.axis_index("outer")
    i = lax.axis_index("inner")
    y = o // 4
    xh = (o // 2) % 2
    c = o % 2
    xl = i // 8
    z = i % 8
    x = xh * 2 + xl
    par = y % 2
    is_a = c == xl
    is_b = c != xl
    own_col = pl.multiple_of(par * SHARE, T)
    give_col = pl.multiple_of(par * CARRY, T)
    take_col = pl.multiple_of((1 - par) * CARRY, T)

    def device(x_, y_, z_, c_):
        return ((y_ * 2 + x_ // 2) * 2 + c_, (x_ % 2) * 8 + z_)

    def along_x(step):
        return device((x + step + 4) % 4, y, z, c)

    def along_y(step):
        return device(x, (y + step + 4) % 4, z, c)

    def along_z(step):
        return device(x, y, (z + step + 8) % 8, c)

    sibling = device(x, y, z, 1 - c)

    def owner_device(dy, dx):
        return device((xh if dx == 0 else 1 - xh) * 2 + xl, (y + dy) % 4, z, c)

    def remote(src, dst, ssem, rsem, dev):
        return pltpu.make_async_remote_copy(
            src_ref=src, dst_ref=dst, send_sem=ssem, recv_sem=rsem, device_id=dev, device_id_type=MESH
        )

    loads = [
        pltpu.make_async_copy(src, dst, in_sem.at[n])
        for n, (src, dst) in enumerate(
            ((og_hbm, OG), (q_hbm, Q), (k_hbm, K), (v_hbm, V), (res_hbm, LO))
        )
    ]
    barrier = pltpu.get_barrier_semaphore()
    greet = [along_z(1), along_z(-1), along_x(1), along_x(-1), along_y(1), along_y(-1), sibling]
    greet += [owner_device(2, 0), owner_device(0, 1), owner_device(1, 1), owner_device(2, 1), owner_device(3, 1)]
    for dev in greet:
        pl.semaphore_signal(barrier, inc=1, device_id=dev, device_id_type=MESH)
    for load in loads:
        load.start()

    exps = exps_ref[...]
    scale = jnp.zeros(exps.shape, F32)
    for octave in range(-16, 1):
        scale = scale + jnp.where(exps == octave, 2.0**octave, 0.0)
    spread = (
        lax.broadcasted_iota(jnp.int32, (HD // BLOCK, HD), 1) // BLOCK
        == lax.broadcasted_iota(jnp.int32, (HD // BLOCK, HD), 0)
    ).astype(BF)
    wide = jnp.dot(scale.astype(BF), spread, preferred_element_type=F32)
    block = codes_ref[...].astype(F32) * wide
    block = jnp.concatenate([block, jnp.zeros((RP - RB, HD), F32)], axis=0)
    W[xl * 8 + z] = block.astype(BF)

    pl.semaphore_wait(barrier, len(greet))

    def zz(e):
        return (z + e) % 8

    def rows(half):
        return pl.ds(*SPAN[half])

    def mine(e):
        return c * 8 + zz(e)

    def theirs(e):
        return (1 - c) * 8 + zz(e)

    def z_copy(way, half, step):
        e = (9 - step) % 8 if way == 0 else step - 1
        part = W.at[mine(e), rows(half), pl.ds(own_col, CARRY)]
        return remote(part, part, zs.at[way, half, step - 1], zr.at[way, half, step - 1], along_z(1 - 2 * way))

    def z_arrival(way, half, step):
        e = 8 - step if way == 0 else step
        part = W.at[mine(e), rows(half), pl.ds(own_col, CARRY)]
        return remote(part, part, zs.at[way, half, step - 1], zr.at[way, half, step - 1], along_z(1 - 2 * way))

    def x_copy(e, half):
        part = W.at[mine(e), rows(half), pl.ds(own_col, CARRY)]
        turn = (half + min(e, 8 - e)) % 2
        return remote(part, part, xs.at[e, half], xr.at[e, half], along_x(1 - 2 * turn))

    def y_copy(e, half, way):
        part = W.at[mine(e), rows(half), pl.ds(pl.multiple_of(give_col + 256 * way, T), 256)]
        return remote(part, part, ys.at[e, half, way], yr.at[e, half, way], along_y(1 - 2 * way))

    def y_arrival(e, half, way):
        part = W.at[mine(e), rows(half), pl.ds(pl.multiple_of(take_col + 256 * way, T), 256)]
        return remote(part, part, ys.at[e, half, way], yr.at[e, half, way], along_y(1 - 2 * way))

    def s_copy(e, half, kind, at=mine):
        cols = pl.ds(own_col, CARRY) if kind == 0 else pl.ds(take_col, SHARE)
        part = W.at[at(e), rows(half), cols]
        return remote(part, part, ss.at[e, half, kind], sr.at[e, half, kind], sibling)

    def spread_out(e, half):
        for way in (0, 1):
            y_copy(e, half, way).start()
        s_copy(e, half, 0).start()

    chunks = [
        [(0, 0), (0, 1)],
        [(7, 0), (1, 0)], [(7, 1), (1, 1)], [(6, 0), (2, 0)], [(6, 1), (2, 1)],
        [(5, 0), (3, 0)], [(5, 1), (3, 1)], [(4, 0), (4, 1)],
    ]

    def serve_z(n):
        @pl.when(is_a)
        def _():
            for e, half in chunks[n]:
                way = (0 if half == 0 else 1) if e == 4 else (0 if e > 4 else 1)
                step = 8 - e if way == 0 else e
                z_arrival(way, half, step).wait_recv()
                if step < chain(way, half):
                    z_copy(way, half, step + 1).start()
                x_copy(e, half).start()
                spread_out(e, half)

    def serve_x(n):
        @pl.when(is_b)
        def _():
            for e, half in chunks[n]:
                x_copy(e, half).wait_recv()
                spread_out(e, half)

    def serve_y(n):
        def go():
            for e, half in chunks[n]:
                for way in (0, 1):
                    y_arrival(e, half, way).wait_recv()
                s_copy(e, half, 1).start()

        if n == 0:
            pl.when(is_b)(go)
        else:
            go()

    @pl.when(is_a)
    def _():
        for half in (0, 1):
            for way in (0, 1):
                z_copy(way, half, 1).start()
            x_copy(0, half).start()

    seg = jnp.broadcast_to(seg_ref[...].astype(F32), (TOK, TOK))
    BIAS[...] = jnp.where(seg == seg.T, 0.0, -1e30)
    factor = 1.0 / math.sqrt(T)

    def head_columns(h):
        return pl.ds(pl.multiple_of(h * T, T), T)

    def forward(h, carry):
        cols = head_columns(h)
        s = dot(Q[:, cols], K[:, cols], 1, 1) * factor + BIAS[...]
        s = jnp.exp(s - jnp.max(s, axis=1, keepdims=True))
        p = s * (1.0 / jnp.sum(s, axis=1, keepdims=True))
        PST[h] = p
        ATT[:, cols] = dot(p.astype(BF), V[:, cols], 1, 0).astype(BF)
        return carry

    def og_blocks(kz, carry):
        lane = lanes(TOK)
        for other in (0, 1):
            b = (c if other == 0 else 1 - c) * 8 + kz
            first = (RB * b) // T
            shift = (RB * b) % T
            back = (T - shift) % T
            tiles = [
                pltpu.roll(
                    OG[:, pl.ds(pl.multiple_of(jnp.minimum(first + n, D // T - 1) * T, T), T)].astype(F32), back, 1
                )
                for n in range(3)
            ]
            left = jnp.where(lane < T - shift, tiles[0], tiles[1]).astype(BF)
            right = jnp.where(lane < T - shift, tiles[1], tiles[2])
            right = jnp.where(lane < RB - T, right, 0.0).astype(BF)
            if other == 0:
                OGR[kz, 0:TOK, 0:T] = left
                OGR[kz, 0:TOK, T : 2 * T] = right
            else:
                OGS[kz, :, 0:T] = left
                OGS[kz, :, T : 2 * T] = right
        return carry

    og_share = remote(OGS, OGR.at[:, pl.ds(TOK, TOK), :], cs.at[0], cr.at[0], sibling)
    at_share = remote(ATR.at[pl.ds(0, TOK), :], ATR.at[pl.ds(TOK, TOK), :], cs.at[1], cr.at[1], sibling)

    pieces = []
    for j in range(8):
        pos = (j // 2 % 2) * 9 + (j // 4) * 2 + j % 2
        pieces.append((pos * T, 208 * j, T))
        pieces.append((SHARE + 80 * j, 208 * j + T, 80))

    def order_columns(n, carry):
        size = 64
        block_rows = pl.ds(pl.multiple_of(n * size, size), size)
        lane = lanes(size)
        done = {}
        for dst, src, length in pieces:
            for t in range(dst // T, (dst + length - 1) // T + 1):
                for u in range(src // T, (src + length - 1) // T + 1):
                    low = max(dst, t * T, dst + T * u - src) - t * T
                    high = min(dst + length, (t + 1) * T, dst + T * (u + 1) - src) - t * T
                    if low >= high:
                        continue
                    tile = ATT[block_rows, u * T : (u + 1) * T].astype(F32)
                    shift = (dst - src) % T
                    if shift:
                        tile = pltpu.roll(tile, shift, 1)
                    if t in done:
                        tile = jnp.where((lane >= low) & (lane < high), tile, done[t])
                    done[t] = tile
        for t, tile in done.items():
            ATR[block_rows, t * T : (t + 1) * T] = tile.astype(BF)
        return carry

    def place(n):
        return (4 + ((n + 1) // 2) * (2 * (n % 2) - 1)) % 8

    def gy_copy(e, way):
        return remote(
            PG.at[zz(e), :, pl.ds(pl.multiple_of(take_col + 256 * way, T), 256)],
            YR.at[e, :, pl.ds(256 * way, 256)],
            gys.at[e, way], gyr.at[e, way], along_y(1 - 2 * way),
        )

    def partial_product(n, carry):
        e = place(n)
        for start, size in ((0, 512), (512, 640), (1152, 512)):
            prod = dot(OGR[zz(e), :, 0:RP], ATR[:, start : start + size], 0, 0)
            PG[zz(e), :, start : start + size] = prod.astype(BF)
        for way in (0, 1):
            gy_copy(e, way).start()
        return carry

    def gx_copy(e, half):
        turn = (half + jnp.minimum(e, 8 - e)) % 2
        return remote(
            PG.at[zz(e), rows(half), pl.ds(own_col, CARRY)],
            XR.at[e, rows(half), :],
            gxs.at[e, half], gxr.at[e, half], along_x(1 - 2 * turn),
        )

    def add_y(n, carry):
        e = place(n)
        for way in (0, 1):
            gy_copy(e, way).wait_recv()
        cols = pl.ds(give_col, SHARE)
        PG[zz(e), :, cols] = (PG[zz(e), :, cols].astype(F32) + YR[e].astype(F32)).astype(BF)

        @pl.when(is_b)
        def _():
            for half in (0, 1):
                gx_copy(e, half).start()

        return carry

    def add_x(n, carry):
        @pl.when(is_a)
        def _():
            e = place(n)
            for half in (0, 1):
                gx_copy(e, half).wait_recv()
            cols = pl.ds(own_col, CARRY)
            PG[zz(e), :, cols] = (PG[zz(e), :, cols].astype(F32) + XR[e].astype(F32)).astype(BF)

        return carry

    def gz_copy(way, half, reach):
        e = reach if way == 0 else 8 - reach
        return remote(
            PG.at[zz(e), rows(half), pl.ds(own_col, CARRY)],
            ZR.at[way, reach - 1, rows(half), :],
            gzs.at[way, half, reach - 1], gzr.at[way, half, reach - 1], along_z(1 - 2 * way),
        )

    def serve_gz(reach):
        @pl.when(is_a)
        def _():
            for half in (0, 1):
                for way in (0, 1):
                    top = chain(way, half)
                    if reach > top:
                        continue
                    if reach < top:
                        gz_copy(way, half, reach + 1).wait_recv()
                        e = (reach if way == 0 else 8 - reach) % 8
                        span = rows(half)
                        cols = pl.ds(own_col, CARRY)
                        PG[zz(e), span, cols] = (
                            PG[zz(e), span, cols].astype(F32) + ZR[way, reach, span, :].astype(F32)
                        ).astype(BF)
                    if reach > 0:
                        gz_copy(way, half, reach).start()

    turns = [(dy, dx) for dy in range(4) for dx in range(2)][1:]

    def owner(dy, dx):
        return (((y + dy) % 4) * 2 + (xh if dx == 0 else 1 - xh))

    def f_copy(dy, dx):
        slot = 2 * dy + dx
        size = 256 if dy % 2 == 0 else T
        return remote(
            LB.at[owner(dy, dx), :, pl.ds(0, size)],
            FR.at[slot, :, pl.ds(0, size)],
            fs.at[slot], fr.at[slot], owner_device(dy, dx),
        )

    def send_last():
        for j in range(8):
            u, shift = divmod(80 * j, T)
            tile = PG[z, :, SHARE + u * T : SHARE + (u + 1) * T].astype(F32)
            if shift:
                tile = pltpu.roll(tile, T - shift, 1)
            if shift + 80 > T:
                more = PG[z, :, SHARE + (u + 1) * T : SHARE + (u + 2) * T].astype(F32)
                tile = jnp.where(lanes(RP) < T - shift, tile, pltpu.roll(more, T - shift, 1))
            LB[j, :, 0:T] = tile.astype(BF)
        for m in range(4):
            j = (m // 2) * 4 + m % 2 + 2 * par
            LB[j, :, T : 2 * T] = PG[z, :, pl.ds(pl.multiple_of(par * CARRY + m * T, T), T)]
        for dy, dx in turns:
            f_copy(dy, dx).start()

    share = remote(SS, SR, cs.at[2], cr.at[2], sibling)

    def finish():
        me = owner(0, 0)
        rest = LB[me, :, 0:T].astype(F32)
        main = LB[me, :, T : 2 * T].astype(F32)
        for dy, dx in turns:
            f_copy(dy, dx).wait_recv()
            rest = rest + FR[2 * dy + dx, :, 0:T].astype(F32)
            if dy % 2 == 0:
                main = main + FR[2 * dy + dx, :, T : 2 * T].astype(F32)
        norm = 1.0 / math.sqrt(TOK * 256)
        main = main * norm
        rest = rest * norm
        second = jnp.where(lanes(RP) < 24, pltpu.roll(main, 24, 1), pltpu.roll(rest, 24, 1))
        SS[...] = jnp.where(c == 0, second, main)
        share.start()
        wg_ref[...] = jnp.where(c == 0, main, second)[0:RB, 0:104]

    def grad_in(kz, carry):
        for start, size in ((0, 512), (512, 640), (1152, 512)):
            cols = pl.ds(start, size)
            AGF[:, cols] += dot(OGR[kz, 0:TOK, 0:RP], W[c * 8 + kz, :, cols], 1, 0) + dot(
                OGS[kz, :, 0:RP], W[(1 - c) * 8 + kz, :, cols], 1, 0
            )
        return carry

    def project(b, carry):
        prod = dot(ATT[...], W[b], 1, 1)
        lane = lanes(TOK)
        first = (RB * b) // T
        shift = (RB * b) % T
        one = pltpu.roll(prod[:, 0:T], shift, 1)
        tail = jnp.concatenate([prod[:, T:RP], jnp.zeros((TOK, 2 * T - RP), F32)], axis=1)
        two = pltpu.roll(tail, shift, 1)

        def put(n, mask, value):
            cols = pl.ds(pl.multiple_of(jnp.minimum(first + n, D // T - 1) * T, T), T)
            old = LO[:, cols]
            new = (old.astype(F32) + value).astype(BF)
            LO[:, cols] = jnp.where(mask, new, old)

        put(0, lane >= shift, one)
        put(1, lane - shift < RB - T, jnp.where(lane < shift, one, two))
        put(2, lane < shift - (2 * T - RB), two)
        return carry

    def backward(h, carry):
        cols = head_columns(h)
        p = PST[h]
        dout = AGB[:, cols]
        q, k, v = Q[:, cols], K[:, cols], V[:, cols]
        delta = jnp.sum(dout.astype(F32) * ATT[:, cols].astype(F32), axis=1, keepdims=True)
        ds = (p * (dot(dout, v, 1, 1) - delta)).astype(BF)
        V[:, cols] = dot(p.astype(BF), dout, 0, 0).astype(BF)
        Q[:, cols] = (dot(ds, k, 1, 0) * factor).astype(BF)
        K[:, cols] = (dot(ds, q, 0, 0) * factor).astype(BF)
        return carry

    def loop(low, high, what):
        lax.fori_loop(low, high, what, 0)

    for load in loads:
        load.wait()
    loop(0, 8, og_blocks)
    og_share.start()
    loop(0, 4, forward)
    serve_z(1)
    serve_x(0)
    loop(4, 8, forward)
    serve_z(2)
    serve_x(1)
    loop(8, 13, forward)
    loop(0, 4, order_columns)
    at_share.start()
    serve_z(3)
    serve_x(2)
    serve_y(0)
    serve_y(1)
    og_share.wait()
    at_share.wait()
    loop(0, 2, partial_product)
    serve_z(4)
    serve_x(3)
    serve_y(2)
    loop(2, 4, partial_product)
    serve_z(5)
    serve_x(4)
    serve_y(3)
    loop(4, 6, partial_product)
    serve_z(6)
    serve_x(5)
    serve_y(4)
    loop(6, 8, partial_product)
    serve_z(7)
    serve_x(6)
    serve_y(5)
    AGF[...] = jnp.zeros((TOK, HD), F32)
    loop(0, 2, add_y)
    serve_x(7)
    serve_y(6)
    loop(2, 4, add_y)
    serve_y(7)

    for n in range(8):
        for e, half in chunks[n]:
            for kind in (0, 1):
                if e == 0:
                    @pl.when(is_a)
                    def _():
                        s_copy(e, half, kind, theirs).wait_recv()
                else:
                    s_copy(e, half, kind, theirs).wait_recv()

    loop(0, 1, add_x)
    serve_gz(4)
    loop(0, 4, grad_in)
    loop(4, 5, add_y)
    loop(1, 3, add_x)
    serve_gz(3)
    loop(4, 8, grad_in)
    AGB[...] = AGF[...].astype(BF)
    loop(5, 6, add_y)
    loop(0, 4, backward)
    loop(6, 8, add_y)
    loop(3, 5, add_x)
    serve_gz(2)
    loop(4, 8, backward)
    loop(5, 7, add_x)
    serve_gz(1)
    loop(8, 13, backward)
    outs = [
        pltpu.make_async_copy(src, dst, out_sem.at[n])
        for n, (src, dst) in enumerate(((Q, dq_hbm), (K, dk_hbm), (V, dv_hbm), (LO, lo_hbm)))
    ]
    for n in range(3):
        outs[n].start()
    loop(7, 8, add_x)
    serve_gz(0)
    pl.when(is_a)(send_last)
    loop(0, 16, project)
    outs[3].start()
    pl.when(is_a)(finish)

    @pl.when(is_b)
    def _():
        share.wait_recv()
        wg_ref[...] = SR[0:RB, 0:104]

    for n in range(8):
        for e, half in chunks[n]:
            def sent(e=e, half=half):
                for way in (0, 1):
                    y_copy(e, half, way).wait_send()
                for kind in (0, 1):
                    s_copy(e, half, kind).wait_send()

            if e == 0:
                pl.when(is_b)(sent)
            else:
                sent()

    def sent_y(e, carry):
        for way in (0, 1):
            gy_copy(e, way).wait_send()
        return carry

    loop(0, 8, sent_y)

    @pl.when(is_b)
    def _():
        def sent_x(e, carry):
            for half in (0, 1):
                gx_copy(e, half).wait_send()
            return carry

        loop(0, 8, sent_x)

    @pl.when(is_a)
    def _():
        for e in range(8):
            for half in (0, 1):
                x_copy(e, half).wait_send()
        for half in (0, 1):
            for way in (0, 1):
                for step in range(1, chain(way, half) + 1):
                    z_copy(way, half, step).wait_send()
                    gz_copy(way, half, step).wait_send()
        for dy, dx in turns:
            f_copy(dy, dx).wait_send()
        share.wait_send()

    for out in outs:
        out.wait()


def block_step(residual_in, queries, keys, values, segment_ids, weight_codes, weight_exponents, out_grad):
    vmem = pl.BlockSpec(memory_space=pltpu.VMEM)
    hbm = pl.BlockSpec(memory_space=pl.ANY)
    dma = pltpu.SemaphoreType.DMA
    V = pltpu.VMEM
    layer_out, query_grad, key_grad, value_grad, weight_grad = pl.pallas_call(
        body_kernel,
        out_shape=(
            jax.ShapeDtypeStruct((TOK, D), BF),
            jax.ShapeDtypeStruct((TOK, HD), BF),
            jax.ShapeDtypeStruct((TOK, HD), BF),
            jax.ShapeDtypeStruct((TOK, HD), BF),
            jax.ShapeDtypeStruct((RB, 104), F32),
        ),
        in_specs=[vmem] * 3 + [hbm] * 5,
        out_specs=(hbm, hbm, hbm, hbm, vmem),
        scratch_shapes=[
            V((16, RP, HD), BF),
            V((8, RP, HD), BF),
            V((8, RP, SHARE), BF),
            V((8, RP, CARRY), BF),
            V((2, 4, RP, CARRY), BF),
            V((8, RP, 2 * T), BF),
            V((8, RP, 2 * T), BF),
            V((RP, T), F32),
            V((RP, T), F32),
            V((8, 2 * TOK, 2 * T), BF),
            V((8, TOK, 2 * T), BF),
            V((2 * TOK, HD), BF),
            V((TOK, HD), BF),
            V((HEADS, TOK, TOK), F32),
            V((TOK, HD), F32),
            V((TOK, HD), BF),
            V((TOK, HD), BF),
            V((TOK, HD), BF),
            V((TOK, HD), BF),
            V((TOK, D), BF),
            V((TOK, D), BF),
            V((TOK, TOK), F32),
            dma((5,)), dma((4,)),
            dma((2, 2, 4)), dma((2, 2, 4)),
            dma((8, 2)), dma((8, 2)),
            dma((8, 2, 2)), dma((8, 2, 2)),
            dma((8, 2, 2)), dma((8, 2, 2)),
            dma((8, 2)), dma((8, 2)),
            dma((8, 2)), dma((8, 2)),
            dma((2, 2, 4)), dma((2, 2, 4)),
            dma((8,)), dma((8,)),
            dma((3,)), dma((3,)),
        ],
        compiler_params=pltpu.CompilerParams(
            collective_id=0, has_side_effects=True, vmem_limit_bytes=60 * 2**20
        ),
        cost_estimate=pl.CostEstimate(flops=10**10, bytes_accessed=2 * 10**7, transcendentals=10**6),
    )(segment_ids, weight_codes, weight_exponents, queries, keys, values, out_grad, residual_in)
    return layer_out, query_grad, key_grad, value_grad, weight_grad


def solution(mesh):
    tokens = P(("outer", "inner"), None)
    in_specs = (tokens, tokens, tokens, tokens, tokens, P("inner", None), P("inner", None), tokens)
    out_specs = (tokens, tokens, tokens, tokens, P("inner", "outer"))
    return jax.shard_map(block_step, mesh=mesh, in_specs=in_specs, out_specs=out_specs, check_vma=False)
```

```python
import functools
import math

import jax
import jax.numpy as jnp
from jax import lax
from jax.experimental import pallas as pl
from jax.experimental.pallas import tpu as pltpu
from jax.sharding import PartitionSpec as P

MESH = pl.DeviceIdType.MESH
BF = jnp.bfloat16
F32 = jnp.float32

TOK = 256
D = 3200
HD = 1664
HEADS = 13
BLOCK = 32
T = 128
RB = 200
RP = 208
SPAN = ((0, 112), (112, 96))
CARRY = 1152
SHARE = 512
TOP = (4, 3)

PLAN = (
    ("load", 4), ("load", 6), ("og", 0, 4), ("load", 5), ("load", 3), ("fwd", 0, 2), ("og", 4, 8), ("fwd", 2, 4),
    ("zero",), ("fwd", 4, 6), ("ogs",), ("Z", 1), ("Z", 2), ("fwd", 6, 8), ("fwd", 8, 10), ("Z", 3), ("YA", 1),
    ("fwd", 10, 12), ("load", 7), ("fwd", 12, 13), ("ord",), ("X", 0), ("Z", 4), ("ats",), ("X", 1), ("shares",),
    ("YA", 2), ("part", 0, 1), ("YA", 3), ("part", 1, 2), ("X", 2), ("YA", 4), ("Z", 5), ("X", 3), ("ay", 0, 1),
    ("Z", 6), ("S", 0), ("part", 2, 3), ("ax", 0, 1), ("E", 1, 0), ("gz", 4), ("S", 1), ("YB", 0), ("YA", 5),
    ("YB", 1), ("X", 4), ("G", 1, 0), ("ay", 1, 2), ("S", 2), ("part", 3, 4), ("YB", 2), ("G", 1, 1), ("E", 1, 1),
    ("ay", 2, 3), ("YB", 3), ("ax", 1, 2), ("part", 4, 5), ("ax", 2, 3), ("Z", 7), ("YA", 6), ("S", 3), ("YB", 4),
    ("gz", 3), ("S", 4), ("X", 5), ("part", 5, 6), ("ay", 3, 4), ("G", 0, 1), ("E", 0, 1), ("ax", 3, 4), ("S", 5),
    ("G", 0, 2), ("E", 1, 2), ("X", 6), ("part", 6, 7), ("ay", 4, 5), ("S", 6), ("YB", 5), ("E", 0, 2), ("E", 1, 3),
    ("YB", 6), ("ax", 4, 5), ("gz", 2), ("E", 0, 3), ("ay", 5, 6), ("X", 7), ("ay", 6, 7), ("part", 7, 8),
    ("ax", 5, 6), ("YA", 7), ("YB", 7), ("G", 0, 3), ("G", 0, 0), ("S", 7), ("E", 0, 4), ("E", 1, 4), ("ax", 6, 7),
    ("gz", 1), ("ay", 7, 8), ("G", 1, 4), ("E", 0, 0), ("round",), ("bwd", 0, 2), ("ax", 7, 8), ("bwd", 2, 4),
    ("bwd", 4, 6), ("G", 1, 3), ("gz", 0), ("last",), ("bwd", 6, 8), ("bwd", 8, 10), ("bwd", 10, 12), ("G", 1, 2),
    ("G", 0, 4), ("fin",), ("bwd", 12, 13),
)


def chain(way, half):
    return TOP[half] if way == 0 else TOP[1 - half]


def dot(a, b, ca, cb):
    return lax.dot_general(a, b, (((ca,), (cb,)), ((), ())), preferred_element_type=F32)


def lanes(rows):
    return lax.broadcasted_iota(jnp.int32, (rows, T), 1)


def body_kernel(
    seg_hbm, codes_hbm, exps_hbm, q_hbm, k_hbm, v_hbm, og_hbm, res_hbm,
    LO, Q, K, V, wg_ref,
    W, PG, YR, XR, ZR, LB, FR, SR, SS, OGR, OGS, ATR, ATT, PST, AGF, AGB, OG, BIAS, CODES, EXPS, SEG,
    in_sem, zs, zr, xs, xr, ys, yr, ss, sr, gys, gyr, gxs, gxr, gzs, gzr, fs, fr, cs, cr,
):
    o = lax.axis_index("outer")
    i = lax.axis_index("inner")
    y = o // 4
    xh = (o // 2) % 2
    c = o % 2
    xl = i // 8
    z = i % 8
    x = xh * 2 + xl
    par = y % 2
    is_a = c == xl
    is_b = c != xl
    own_col = pl.multiple_of(par * SHARE, T)
    give_col = pl.multiple_of(par * CARRY, T)
    take_col = pl.multiple_of((1 - par) * CARRY, T)

    def device(x_, y_, z_, c_):
        return ((y_ * 2 + x_ // 2) * 2 + c_, (x_ % 2) * 8 + z_)

    def along_x(step):
        return device((x + step + 4) % 4, y, z, c)

    def along_y(step):
        return device(x, (y + step + 4) % 4, z, c)

    def along_z(step):
        return device(x, y, (z + step + 8) % 8, c)

    sibling = device(x, y, z, 1 - c)

    def owner_device(dy, dx):
        return device((xh if dx == 0 else 1 - xh) * 2 + xl, (y + dy) % 4, z, c)

    def remote(src, dst, ssem, rsem, dev):
        return pltpu.make_async_remote_copy(
            src_ref=src, dst_ref=dst, send_sem=ssem, recv_sem=rsem, device_id=dev, device_id_type=MESH
        )

    barrier = pltpu.get_barrier_semaphore()
    greet = [along_z(1), along_z(-1), along_x(1), along_x(-1), along_y(1), along_y(-1), sibling]
    greet += [owner_device(2, 0), owner_device(0, 1), owner_device(1, 1), owner_device(2, 1), owner_device(3, 1)]
    for dev in greet:
        pl.semaphore_signal(barrier, inc=1, device_id=dev, device_id_type=MESH)
    loads = [
        pltpu.make_async_copy(src, dst, in_sem.at[n])
        for n, (src, dst) in enumerate(
            ((codes_hbm, CODES), (exps_hbm, EXPS), (seg_hbm, SEG), (q_hbm, Q), (k_hbm, K), (v_hbm, V), (og_hbm, OG), (res_hbm, LO))
        )
    ]
    for load in loads:
        load.start()

    for n in range(3):
        loads[n].wait()
    exps = EXPS[...]
    scale = jnp.zeros(exps.shape, F32)
    for octave in range(-16, 1):
        scale = scale + jnp.where(exps == octave, 2.0**octave, 0.0)
    spread = (
        lax.broadcasted_iota(jnp.int32, (HD // BLOCK, HD), 1) // BLOCK
        == lax.broadcasted_iota(jnp.int32, (HD // BLOCK, HD), 0)
    ).astype(BF)
    wide = dot(scale.astype(BF), spread, 0, 0)
    block = CODES[...].astype(F32) * wide
    block = jnp.concatenate([block, jnp.zeros((RP - RB, HD), F32)], axis=0)
    W[xl * 8 + z] = block.astype(BF)

    pl.semaphore_wait(barrier, len(greet))

    def zz(e):
        return (z + e) % 8

    def rows(half):
        return pl.ds(*SPAN[half])

    def mine(e):
        return c * 8 + zz(e)

    def theirs(e):
        return (1 - c) * 8 + zz(e)

    def z_copy(way, half, step):
        e = (9 - step) % 8 if way == 0 else step - 1
        part = W.at[mine(e), rows(half), pl.ds(own_col, CARRY)]
        return remote(part, part, zs.at[way, half, step - 1], zr.at[way, half, step - 1], along_z(1 - 2 * way))

    def z_arrival(way, half, step):
        e = 8 - step if way == 0 else step
        part = W.at[mine(e), rows(half), pl.ds(own_col, CARRY)]
        return remote(part, part, zs.at[way, half, step - 1], zr.at[way, half, step - 1], along_z(1 - 2 * way))

    def x_copy(e, half):
        part = W.at[mine(e), rows(half), pl.ds(own_col, CARRY)]
        turn = (half + min(e, 8 - e)) % 2
        return remote(part, part, xs.at[e, half], xr.at[e, half], along_x(1 - 2 * turn))

    def y_copy(e, half, way):
        part = W.at[mine(e), rows(half), pl.ds(pl.multiple_of(give_col + 256 * way, T), 256)]
        return remote(part, part, ys.at[e, half, way], yr.at[e, half, way], along_y(1 - 2 * way))

    def y_arrival(e, half, way):
        part = W.at[mine(e), rows(half), pl.ds(pl.multiple_of(take_col + 256 * way, T), 256)]
        return remote(part, part, ys.at[e, half, way], yr.at[e, half, way], along_y(1 - 2 * way))

    def s_copy(e, half, kind, at=mine):
        cols = pl.ds(own_col, CARRY) if kind == 0 else pl.ds(take_col, SHARE)
        part = W.at[at(e), rows(half), cols]
        return remote(part, part, ss.at[e, half, kind], sr.at[e, half, kind], sibling)

    def spread_out(e, half):
        for way in (0, 1):
            y_copy(e, half, way).start()
        s_copy(e, half, 0).start()

    chunks = [
        [(0, 0), (0, 1)],
        [(7, 0), (1, 0)], [(7, 1), (1, 1)], [(6, 0), (2, 0)], [(6, 1), (2, 1)],
        [(5, 0), (3, 0)], [(5, 1), (3, 1)], [(4, 0), (4, 1)],
    ]

    def serve_z(n):
        @pl.when(is_a)
        def _():
            for e, half in chunks[n]:
                way = (0 if half == 0 else 1) if e == 4 else (0 if e > 4 else 1)
                step = 8 - e if way == 0 else e
                z_arrival(way, half, step).wait_recv()
                if step < chain(way, half):
                    z_copy(way, half, step + 1).start()
                x_copy(e, half).start()
                spread_out(e, half)

    def serve_x(n):
        @pl.when(is_b)
        def _():
            for e, half in chunks[n]:
                x_copy(e, half).wait_recv()
                spread_out(e, half)

    def serve_y(n, role):
        @pl.when(role)
        def _():
            for e, half in chunks[n]:
                for way in (0, 1):
                    y_arrival(e, half, way).wait_recv()
                s_copy(e, half, 1).start()

    @pl.when(is_a)
    def _():
        for half in (0, 1):
            for way in (0, 1):
                z_copy(way, half, 1).start()
            x_copy(0, half).start()

    seg = jnp.broadcast_to(SEG[...].astype(F32), (TOK, TOK))
    BIAS[...] = jnp.where(seg == seg.T, 0.0, -1e30)
    factor = 1.0 / math.sqrt(T)

    def head_columns(h):
        return pl.ds(pl.multiple_of(h * T, T), T)

    def forward(h, carry):
        cols = head_columns(h)
        s = dot(Q[:, cols], K[:, cols], 1, 1) * factor + BIAS[...]
        s = jnp.exp(s - jnp.max(s, axis=1, keepdims=True))
        p = s * (1.0 / jnp.sum(s, axis=1, keepdims=True))
        PST[h] = p
        ATT[:, cols] = dot(p.astype(BF), V[:, cols], 1, 0).astype(BF)
        return carry

    def og_blocks(kz, carry):
        lane = lanes(TOK)
        for other in (0, 1):
            b = (c if other == 0 else 1 - c) * 8 + kz
            first = (RB * b) // T
            shift = (RB * b) % T
            back = (T - shift) % T
            tiles = [
                pltpu.roll(
                    OG[:, pl.ds(pl.multiple_of(jnp.minimum(first + n, D // T - 1) * T, T), T)].astype(F32), back, 1
                )
                for n in range(3)
            ]
            left = jnp.where(lane < T - shift, tiles[0], tiles[1]).astype(BF)
            right = jnp.where(lane < T - shift, tiles[1], tiles[2])
            right = jnp.where(lane < RB - T, right, 0.0).astype(BF)
            if other == 0:
                OGR[kz, 0:TOK, 0:T] = left
                OGR[kz, 0:TOK, T : 2 * T] = right
            else:
                OGS[kz, :, 0:T] = left
                OGS[kz, :, T : 2 * T] = right
        return carry

    og_share = remote(OGS, OGR.at[:, pl.ds(TOK, TOK), :], cs.at[0], cr.at[0], sibling)
    at_share = remote(ATR.at[pl.ds(0, TOK), :], ATR.at[pl.ds(TOK, TOK), :], cs.at[1], cr.at[1], sibling)

    pieces = []
    for j in range(8):
        pos = (j // 2 % 2) * 9 + (j // 4) * 2 + j % 2
        pieces.append((pos * T, 208 * j, T))
        pieces.append((SHARE + 80 * j, 208 * j + T, 80))

    def order_columns(n, carry):
        size = 64
        block_rows = pl.ds(pl.multiple_of(n * size, size), size)
        lane = lanes(size)
        done = {}
        for dst, src, length in pieces:
            for t in range(dst // T, (dst + length - 1) // T + 1):
                for u in range(src // T, (src + length - 1) // T + 1):
                    low = max(dst, t * T, dst + T * u - src) - t * T
                    high = min(dst + length, (t + 1) * T, dst + T * (u + 1) - src) - t * T
                    if low >= high:
                        continue
                    tile = ATT[block_rows, u * T : (u + 1) * T].astype(F32)
                    shift = (dst - src) % T
                    if shift:
                        tile = pltpu.roll(tile, shift, 1)
                    if t in done:
                        tile = jnp.where((lane >= low) & (lane < high), tile, done[t])
                    done[t] = tile
        for t, tile in done.items():
            ATR[block_rows, t * T : (t + 1) * T] = tile.astype(BF)
        return carry

    def place(n):
        return (4 + ((n + 1) // 2) * (2 * (n % 2) - 1)) % 8

    def gy_copy(e, way):
        return remote(
            PG.at[zz(e), :, pl.ds(pl.multiple_of(take_col + 256 * way, T), 256)],
            YR.at[e, :, pl.ds(256 * way, 256)],
            gys.at[e, way], gyr.at[e, way], along_y(1 - 2 * way),
        )

    def partial_product(n, carry):
        e = place(n)
        for start, size in ((0, 512), (512, 640), (1152, 512)):
            prod = dot(OGR[zz(e), :, 0:RP], ATR[:, start : start + size], 0, 0)
            PG[zz(e), :, start : start + size] = prod.astype(BF)
        for way in (0, 1):
            gy_copy(e, way).start()
        return carry

    def gx_copy(e, half):
        turn = (half + jnp.minimum(e, 8 - e)) % 2
        return remote(
            PG.at[zz(e), rows(half), pl.ds(own_col, CARRY)],
            XR.at[e, rows(half), :],
            gxs.at[e, half], gxr.at[e, half], along_x(1 - 2 * turn),
        )

    def add_y(n, carry):
        e = place(n)
        for way in (0, 1):
            gy_copy(e, way).wait_recv()
        cols = pl.ds(give_col, SHARE)
        PG[zz(e), :, cols] = (PG[zz(e), :, cols].astype(F32) + YR[e].astype(F32)).astype(BF)

        @pl.when(is_b)
        def _():
            for half in (0, 1):
                gx_copy(e, half).start()

        return carry

    def add_x(n, carry):
        @pl.when(is_a)
        def _():
            e = place(n)
            for half in (0, 1):
                gx_copy(e, half).wait_recv()
            cols = pl.ds(own_col, CARRY)
            PG[zz(e), :, cols] = (PG[zz(e), :, cols].astype(F32) + XR[e].astype(F32)).astype(BF)

        return carry

    def gz_copy(way, half, reach):
        e = reach if way == 0 else 8 - reach
        return remote(
            PG.at[zz(e), rows(half), pl.ds(own_col, CARRY)],
            ZR.at[way, reach - 1, rows(half), :],
            gzs.at[way, half, reach - 1], gzr.at[way, half, reach - 1], along_z(1 - 2 * way),
        )

    def serve_gz(reach):
        @pl.when(is_a)
        def _():
            for half in (0, 1):
                for way in (0, 1):
                    top = chain(way, half)
                    if reach > top:
                        continue
                    if reach < top:
                        gz_copy(way, half, reach + 1).wait_recv()
                        e = (reach if way == 0 else 8 - reach) % 8
                        span = rows(half)
                        cols = pl.ds(own_col, CARRY)
                        PG[zz(e), span, cols] = (
                            PG[zz(e), span, cols].astype(F32) + ZR[way, reach, span, :].astype(F32)
                        ).astype(BF)
                    if reach > 0:
                        gz_copy(way, half, reach).start()

    turns = [(dy, dx) for dy in range(4) for dx in range(2)][1:]

    def owner(dy, dx):
        return (((y + dy) % 4) * 2 + (xh if dx == 0 else 1 - xh))

    def f_copy(dy, dx):
        slot = 2 * dy + dx
        size = 256 if dy % 2 == 0 else T
        return remote(
            LB.at[owner(dy, dx), :, pl.ds(0, size)],
            FR.at[slot, :, pl.ds(0, size)],
            fs.at[slot], fr.at[slot], owner_device(dy, dx),
        )

    def send_last():
        for j in range(8):
            u, shift = divmod(80 * j, T)
            tile = PG[z, :, SHARE + u * T : SHARE + (u + 1) * T].astype(F32)
            if shift:
                tile = pltpu.roll(tile, T - shift, 1)
            if shift + 80 > T:
                more = PG[z, :, SHARE + (u + 1) * T : SHARE + (u + 2) * T].astype(F32)
                tile = jnp.where(lanes(RP) < T - shift, tile, pltpu.roll(more, T - shift, 1))
            LB[j, :, 0:T] = tile.astype(BF)
        for m in range(4):
            j = (m // 2) * 4 + m % 2 + 2 * par
            LB[j, :, T : 2 * T] = PG[z, :, pl.ds(pl.multiple_of(par * CARRY + m * T, T), T)]
        for dy, dx in turns:
            f_copy(dy, dx).start()

    share = remote(SS, SR, cs.at[2], cr.at[2], sibling)

    def finish():
        me = owner(0, 0)
        rest = LB[me, :, 0:T].astype(F32)
        main = LB[me, :, T : 2 * T].astype(F32)
        for dy, dx in turns:
            f_copy(dy, dx).wait_recv()
            rest = rest + FR[2 * dy + dx, :, 0:T].astype(F32)
            if dy % 2 == 0:
                main = main + FR[2 * dy + dx, :, T : 2 * T].astype(F32)
        norm = 1.0 / math.sqrt(TOK * 256)
        main = main * norm
        rest = rest * norm
        second = jnp.where(lanes(RP) < 24, pltpu.roll(main, 24, 1), pltpu.roll(rest, 24, 1))
        SS[...] = jnp.where(c == 0, second, main)
        share.start()
        wg_ref[...] = jnp.where(c == 0, main, second)[0:RB, 0:104]

    def grad_in(who, e):
        kz = zz(e)
        lhs = OGR[kz, 0:TOK, 0:RP] if who == 0 else OGS[kz, :, 0:RP]
        b = mine(e) if who == 0 else theirs(e)
        for start, size in ((0, 512), (512, 640), (1152, 512)):
            cols = pl.ds(start, size)
            AGF[:, cols] += dot(lhs, W[b, :, cols], 1, 0)

    def project(who, e):
        b = mine(e) if who == 0 else theirs(e)
        prod = dot(ATT[...], W[b], 1, 1)
        lane = lanes(TOK)
        first = (RB * b) // T
        shift = (RB * b) % T
        one = pltpu.roll(prod[:, 0:T], shift, 1)
        tail = jnp.concatenate([prod[:, T:RP], jnp.zeros((TOK, 2 * T - RP), F32)], axis=1)
        two = pltpu.roll(tail, shift, 1)

        def put(n, mask, value):
            cols = pl.ds(pl.multiple_of(jnp.minimum(first + n, D // T - 1) * T, T), T)
            old = LO[:, cols]
            new = (old.astype(F32) + value).astype(BF)
            LO[:, cols] = jnp.where(mask, new, old)

        put(0, lane >= shift, one)
        put(1, lane - shift < RB - T, jnp.where(lane < shift, one, two))
        put(2, lane < shift - (2 * T - RB), two)

    def backward(h, carry):
        cols = head_columns(h)
        p = PST[h]
        dout = AGB[:, cols]
        q, k, v = Q[:, cols], K[:, cols], V[:, cols]
        delta = jnp.sum(dout.astype(F32) * ATT[:, cols].astype(F32), axis=1, keepdims=True)
        ds = (p * (dot(dout, v, 1, 1) - delta)).astype(BF)
        V[:, cols] = dot(p.astype(BF), dout, 0, 0).astype(BF)
        Q[:, cols] = (dot(ds, k, 1, 0) * factor).astype(BF)
        K[:, cols] = (dot(ds, q, 0, 0) * factor).astype(BF)
        return carry

    def loop(low, high, what):
        lax.fori_loop(low, high, what, 0)

    def blocks(what, who, group):
        low = group % 4
        if low == 0:
            what(who, group)
        else:
            def go(n, carry):
                what(who, low + n * (8 - 2 * low))
                return carry

            loop(0, 2, go)

    def serve_s(n):
        for e, half in chunks[n]:
            def go(e=e, half=half):
                for kind in (0, 1):
                    s_copy(e, half, kind, theirs).wait_recv()

            if e == 0:
                pl.when(is_a)(go)
            else:
                go()

    def zero_grad():
        AGF[...] = jnp.zeros((TOK, HD), F32)

    def round_grad():
        AGB[...] = AGF[...].astype(BF)

    def shares():
        og_share.wait()
        at_share.wait()

    does = {
        "load": lambda n: loads[n].wait(),
        "og": lambda a, b: loop(a, b, og_blocks),
        "ogs": og_share.start,
        "fwd": lambda a, b: loop(a, b, forward),
        "ord": lambda: loop(0, 4, order_columns),
        "ats": at_share.start,
        "shares": shares,
        "Z": serve_z, "X": serve_x, "S": serve_s,
        "YA": lambda n: serve_y(n, is_a),
        "YB": lambda n: serve_y(n, is_b),
        "part": lambda a, b: loop(a, b, partial_product),
        "ay": lambda a, b: loop(a, b, add_y),
        "ax": lambda a, b: loop(a, b, add_x),
        "gz": serve_gz,
        "zero": zero_grad,
        "E": lambda who, group: blocks(grad_in, who, group),
        "G": lambda who, group: blocks(project, who, group),
        "round": round_grad,
        "bwd": lambda a, b: loop(a, b, backward),
        "last": lambda: pl.when(is_a)(send_last),
        "fin": lambda: pl.when(is_a)(finish),
    }
    for name, *args in PLAN:
        does[name](*args)

    @pl.when(is_b)
    def _():
        share.wait_recv()
        wg_ref[...] = SR[0:RB, 0:104]

    for n in range(8):
        for e, half in chunks[n]:
            def sent(e=e, half=half):
                for way in (0, 1):
                    y_copy(e, half, way).wait_send()
                for kind in (0, 1):
                    s_copy(e, half, kind).wait_send()

            if e == 0:
                pl.when(is_b)(sent)
            else:
                sent()

    def sent_y(e, carry):
        for way in (0, 1):
            gy_copy(e, way).wait_send()
        return carry

    loop(0, 8, sent_y)

    @pl.when(is_b)
    def _():
        def sent_x(e, carry):
            for half in (0, 1):
                gx_copy(e, half).wait_send()
            return carry

        loop(0, 8, sent_x)

    @pl.when(is_a)
    def _():
        for e in range(8):
            for half in (0, 1):
                x_copy(e, half).wait_send()
        for half in (0, 1):
            for way in (0, 1):
                for step in range(1, chain(way, half) + 1):
                    z_copy(way, half, step).wait_send()
                    gz_copy(way, half, step).wait_send()
        for dy, dx in turns:
            f_copy(dy, dx).wait_send()
        share.wait_send()


def store_kernel(*refs):
    sems = refs[-1]
    copies = [pltpu.make_async_copy(refs[n], refs[5 + n], sems.at[n]) for n in range(5)]
    for copy in copies:
        copy.start()
    for copy in copies:
        copy.wait()


def block_step(residual_in, queries, keys, values, segment_ids, weight_codes, weight_exponents, out_grad):
    vmem = pl.BlockSpec(memory_space=pltpu.VMEM)
    hbm = pl.BlockSpec(memory_space=pl.ANY)
    dma = pltpu.SemaphoreType.DMA
    V = pltpu.VMEM
    shapes = (((TOK, D), BF), ((TOK, HD), BF), ((TOK, HD), BF), ((TOK, HD), BF), ((RB, 104), F32))
    args = (segment_ids, weight_codes, weight_exponents.T, queries, keys, values, out_grad, residual_in)
    args = [pltpu.with_memory_space_constraint(arg, pltpu.HBM) for arg in args]
    outs = pl.pallas_call(
        body_kernel,
        out_shape=tuple(V(*shape) for shape in shapes),
        in_specs=[pl.BlockSpec(memory_space=pltpu.HBM)] * 8,
        out_specs=(vmem,) * 5,
        scratch_shapes=[
            V((16, RP, HD), BF),
            V((8, RP, HD), BF),
            V((8, RP, SHARE), BF),
            V((8, RP, CARRY), BF),
            V((2, 4, RP, CARRY), BF),
            V((8, RP, 2 * T), BF),
            V((8, RP, 2 * T), BF),
            V((RP, T), F32),
            V((RP, T), F32),
            V((8, 2 * TOK, 2 * T), BF),
            V((8, TOK, 2 * T), BF),
            V((2 * TOK, HD), BF),
            V((TOK, HD), BF),
            V((HEADS, TOK, TOK), F32),
            V((TOK, HD), F32),
            V((TOK, HD), BF),
            V((TOK, D), BF),
            V((TOK, TOK), F32),
            V((RB, HD), BF),
            V((HD // BLOCK, RB), jnp.int32),
            V((1, TOK), jnp.int32),
            dma((8,)),
            dma((2, 2, 4)), dma((2, 2, 4)),
            dma((8, 2)), dma((8, 2)),
            dma((8, 2, 2)), dma((8, 2, 2)),
            dma((8, 2, 2)), dma((8, 2, 2)),
            dma((8, 2)), dma((8, 2)),
            dma((8, 2)), dma((8, 2)),
            dma((2, 2, 4)), dma((2, 2, 4)),
            dma((8,)), dma((8,)),
            dma((3,)), dma((3,)),
        ],
        compiler_params=pltpu.CompilerParams(
            collective_id=0, has_side_effects=True, vmem_limit_bytes=48 * 2**20
        ),
        cost_estimate=pl.CostEstimate(flops=10**10, bytes_accessed=2 * 10**7, transcendentals=10**6),
    )(*args)
    outs = [pltpu.with_memory_space_constraint(out, pltpu.VMEM) for out in outs]
    return pl.pallas_call(
        store_kernel,
        out_shape=tuple(jax.ShapeDtypeStruct(*shape) for shape in shapes),
        in_specs=[hbm] * 5,
        out_specs=(hbm,) * 5,
        scratch_shapes=[dma((5,))],
        compiler_params=pltpu.CompilerParams(vmem_limit_bytes=2**20),
    )(*outs)


def solution(mesh):
    tokens = P(("outer", "inner"), None)
    in_specs = (tokens, tokens, tokens, tokens, tokens, P("inner", None), P("inner", None), tokens)
    out_specs = (tokens, tokens, tokens, tokens, P("inner", "outer"))
    return jax.shard_map(block_step, mesh=mesh, in_specs=in_specs, out_specs=out_specs, check_vma=False)
```

```python
import functools
import math

import jax
import jax.numpy as jnp
from jax import lax
from jax.experimental import pallas as pl
from jax.experimental.pallas import tpu as pltpu
from jax.sharding import PartitionSpec as P

MESH = pl.DeviceIdType.MESH
BF = jnp.bfloat16
F32 = jnp.float32

TOK = 256
D = 3200
HD = 1664
HEADS = 13
BLOCK = 32
T = 128
RB = 200
RP = 208
SPAN = ((0, 112), (112, 96))
CARRY = 1152
SHARE = 512
TOP = (4, 3)

GROUPS = ((0,), (7, 1), (6, 2), (5, 3), (4,))

PLAN = (
    ("load", 6), ("load", 3), ("og", 0, 4), ("load", 4), ("load", 5), ("fwd", 0, 2), ("og", 4, 8), ("fwd", 2, 4),
    ("fwd", 4, 6), ("ogs",), ("Z", 1), ("fwd", 6, 8), ("fwd", 8, 10), ("fwd", 10, 12), ("Z", 2), ("fwd", 12, 13),
    ("Z", 3), ("ord",), ("ats",), ("X", 0), ("X", 1), ("shares",), ("part", 0, 1), ("Z", 4), ("zero",),
    ("part", 1, 2), ("part", 2, 3), ("Z", 5), ("ay", 0, 1), ("Z", 6), ("YA", 1), ("part", 3, 4), ("X", 2), ("YA", 2),
    ("load", 7), ("ax", 0, 1), ("YA", 3), ("part", 4, 5), ("YB", 0), ("gz", 4), ("X", 3), ("ay", 1, 2), ("ay", 2, 3),
    ("X", 4), ("S", 0), ("ax", 1, 2), ("ay", 3, 4), ("YB", 1), ("part", 5, 6), ("ay", 4, 5), ("YA", 4),
    ("part", 6, 7), ("ax", 2, 3), ("YB", 2), ("X", 5), ("gz", 3), ("E", 1, 0), ("X", 6), ("E", 0, 1), ("YA", 5),
    ("G", 1, 0), ("YB", 3), ("ay", 5, 6), ("part", 7, 8), ("S", 1), ("ax", 3, 4), ("E", 0, 0), ("Z", 7), ("YB", 4),
    ("ax", 4, 5), ("gz", 2), ("G", 0, 2), ("ay", 6, 7), ("X", 7), ("S", 2), ("E", 0, 2), ("ax", 5, 6), ("YB", 5),
    ("YB", 6), ("YA", 6), ("G", 0, 3), ("S", 3), ("YA", 7), ("S", 4), ("ay", 7, 8), ("ax", 6, 7), ("YB", 7), ("S", 5),
    ("S", 6), ("gz", 1), ("G", 0, 4), ("S", 7), ("E", 1, 3), ("G", 1, 1), ("E", 1, 4), ("G", 0, 0), ("E", 1, 1),
    ("E", 0, 3), ("E", 0, 4), ("G", 0, 1), ("E", 1, 2), ("ax", 7, 8), ("gz", 0), ("last",), ("G", 1, 2), ("G", 1, 4),
    ("round",), ("bwd", 0, 2), ("bwd", 2, 4), ("G", 1, 3), ("bwd", 4, 6), ("bwd", 6, 8), ("bwd", 8, 10),
    ("bwd", 10, 12), ("fin",), ("bwd", 12, 13),
)


def chain(way, half):
    return TOP[half] if way == 0 else TOP[1 - half]


def dot(a, b, ca, cb):
    return lax.dot_general(a, b, (((ca,), (cb,)), ((), ())), preferred_element_type=F32)


def lanes(rows):
    return lax.broadcasted_iota(jnp.int32, (rows, T), 1)


def body_kernel(
    seg_hbm, codes_hbm, exps_hbm, q_hbm, k_hbm, v_hbm, og_hbm, res_hbm,
    LO, Q, K, V, wg_ref,
    W, PG, YR, XR, ZR, LB, FR, SR, SS, OGR, OGS, ATR, ATT, PST, AGF, AGB, OG, BIAS, CODES, EXPS, SEG,
    in_sem, zs, zr, xs, xr, ys, yr, ss, sr, gys, gyr, gxs, gxr, gzs, gzr, fs, fr, cs, cr,
):
    o = lax.axis_index("outer")
    i = lax.axis_index("inner")
    y = o // 4
    xh = (o // 2) % 2
    c = o % 2
    xl = i // 8
    z = i % 8
    x = xh * 2 + xl
    par = y % 2
    is_a = c == xl
    is_b = c != xl
    own_col = pl.multiple_of(par * SHARE, T)
    give_col = pl.multiple_of(par * CARRY, T)
    take_col = pl.multiple_of((1 - par) * CARRY, T)

    def device(x_, y_, z_, c_):
        return ((y_ * 2 + x_ // 2) * 2 + c_, (x_ % 2) * 8 + z_)

    def along_x(step):
        return device((x + step + 4) % 4, y, z, c)

    def along_y(step):
        return device(x, (y + step + 4) % 4, z, c)

    def along_z(step):
        return device(x, y, (z + step + 8) % 8, c)

    sibling = device(x, y, z, 1 - c)

    def owner_device(dy, dx):
        return device((xh if dx == 0 else 1 - xh) * 2 + xl, (y + dy) % 4, z, c)

    def remote(src, dst, ssem, rsem, dev):
        return pltpu.make_async_remote_copy(
            src_ref=src, dst_ref=dst, send_sem=ssem, recv_sem=rsem, device_id=dev, device_id_type=MESH
        )

    loads = [
        pltpu.make_async_copy(src, dst, in_sem.at[n])
        for n, (src, dst) in enumerate(
            ((codes_hbm, CODES), (exps_hbm, EXPS), (seg_hbm, SEG), (q_hbm, Q), (k_hbm, K), (v_hbm, V), (og_hbm, OG), (res_hbm, LO))
        )
    ]
    for load in loads[:3]:
        load.start()
    barrier = pltpu.get_barrier_semaphore()
    greet = [along_z(1), along_z(-1), along_x(1), along_x(-1), along_y(1), along_y(-1), sibling]
    greet += [owner_device(2, 0), owner_device(0, 1), owner_device(1, 1), owner_device(2, 1), owner_device(3, 1)]
    for dev in greet:
        pl.semaphore_signal(barrier, inc=1, device_id=dev, device_id_type=MESH)

    for load in loads[3:]:
        load.start()
    for load in loads[:3]:
        load.wait()
    exps = EXPS[...]
    scale = jnp.zeros(exps.shape, F32)
    for octave in range(-16, 1):
        scale = scale + jnp.where(exps == octave, 2.0**octave, 0.0)
    spread = (
        lax.broadcasted_iota(jnp.int32, (HD // BLOCK, HD), 1) // BLOCK
        == lax.broadcasted_iota(jnp.int32, (HD // BLOCK, HD), 0)
    ).astype(BF)
    wide = dot(scale.astype(BF), spread, 0, 0)
    block = CODES[...].astype(F32) * wide
    block = jnp.concatenate([block, jnp.zeros((RP - RB, HD), F32)], axis=0)
    W[xl * 8 + z] = block.astype(BF)

    pl.semaphore_wait(barrier, len(greet))

    def zz(e):
        return (z + e) % 8

    def rows(half):
        return pl.ds(*SPAN[half])

    def mine(e):
        return c * 8 + zz(e)

    def theirs(e):
        return (1 - c) * 8 + zz(e)

    def z_copy(way, half, step):
        e = (9 - step) % 8 if way == 0 else step - 1
        part = W.at[mine(e), rows(half), pl.ds(own_col, CARRY)]
        return remote(part, part, zs.at[way, half, step - 1], zr.at[way, half, step - 1], along_z(1 - 2 * way))

    def z_arrival(way, half, step):
        e = 8 - step if way == 0 else step
        part = W.at[mine(e), rows(half), pl.ds(own_col, CARRY)]
        return remote(part, part, zs.at[way, half, step - 1], zr.at[way, half, step - 1], along_z(1 - 2 * way))

    def x_copy(e, half):
        part = W.at[mine(e), rows(half), pl.ds(own_col, CARRY)]
        turn = (half + min(e, 8 - e)) % 2
        return remote(part, part, xs.at[e, half], xr.at[e, half], along_x(1 - 2 * turn))

    def y_copy(e, half, way):
        part = W.at[mine(e), rows(half), pl.ds(pl.multiple_of(give_col + 256 * way, T), 256)]
        return remote(part, part, ys.at[e, half, way], yr.at[e, half, way], along_y(1 - 2 * way))

    def y_arrival(e, half, way):
        part = W.at[mine(e), rows(half), pl.ds(pl.multiple_of(take_col + 256 * way, T), 256)]
        return remote(part, part, ys.at[e, half, way], yr.at[e, half, way], along_y(1 - 2 * way))

    def s_copy(e, half, kind, at=mine):
        cols = pl.ds(own_col, CARRY) if kind == 0 else pl.ds(take_col, SHARE)
        part = W.at[at(e), rows(half), cols]
        return remote(part, part, ss.at[e, half, kind], sr.at[e, half, kind], sibling)

    def spread_out(e, half):
        for way in (0, 1):
            y_copy(e, half, way).start()
        s_copy(e, half, 0).start()

    chunks = [
        [(0, 0), (0, 1)],
        [(7, 0), (1, 0)], [(7, 1), (1, 1)], [(6, 0), (2, 0)], [(6, 1), (2, 1)],
        [(5, 0), (3, 0)], [(5, 1), (3, 1)], [(4, 0), (4, 1)],
    ]

    def serve_z(n):
        @pl.when(is_a)
        def _():
            for e, half in chunks[n]:
                way = (0 if half == 0 else 1) if e == 4 else (0 if e > 4 else 1)
                step = 8 - e if way == 0 else e
                z_arrival(way, half, step).wait_recv()
                if step < chain(way, half):
                    z_copy(way, half, step + 1).start()
                if e != 4:
                    x_copy(e, half).start()
                spread_out(e, half)

    def serve_x(n):
        @pl.when(is_b)
        def _():
            for e, half in chunks[n]:
                if e == 4:
                    z_arrival(half, half, 4).wait_recv()
                else:
                    x_copy(e, half).wait_recv()
                if (e, half) in ((5, 0), (3, 1)):
                    z_copy(half, half, 4).start()
                spread_out(e, half)

    def serve_y(n, role):
        @pl.when(role)
        def _():
            for e, half in chunks[n]:
                for way in (0, 1):
                    y_arrival(e, half, way).wait_recv()
                s_copy(e, half, 1).start()

    @pl.when(is_a)
    def _():
        for half in (0, 1):
            for way in (0, 1):
                z_copy(way, half, 1).start()
            x_copy(0, half).start()

    seg = jnp.broadcast_to(SEG[...].astype(F32), (TOK, TOK))
    BIAS[...] = jnp.where(seg == seg.T, 0.0, -1e30)
    factor = 1.0 / math.sqrt(T)

    def head_columns(h):
        return slice(h * T, (h + 1) * T)

    def forward(low, high):
        cols = [head_columns(h) for h in range(low, high)]
        qs, ks, vs = [[ref[:, col] for col in cols] for ref in (Q, K, V)]
        bias = BIAS[...]
        scores = [dot(q, k, 1, 1) * factor + bias for q, k in zip(qs, ks)]
        tops = [jnp.max(s, axis=1, keepdims=True) for s in scores]
        scores = [jnp.exp(s - top) for s, top in zip(scores, tops)]
        sums = [1.0 / jnp.sum(s, axis=1, keepdims=True) for s in scores]
        probs = [s * inverse for s, inverse in zip(scores, sums)]
        outs = [dot(p.astype(BF), v, 1, 0).astype(BF) for p, v in zip(probs, vs)]
        for n, h in enumerate(range(low, high)):
            PST[h] = probs[n]
            ATT[:, cols[n]] = outs[n]

    def og_blocks(kz, carry):
        lane = lanes(TOK)
        for other in (0, 1):
            b = (c if other == 0 else 1 - c) * 8 + kz
            first = (RB * b) // T
            shift = (RB * b) % T
            back = (T - shift) % T
            tiles = [
                pltpu.roll(
                    OG[:, pl.ds(pl.multiple_of(jnp.minimum(first + n, D // T - 1) * T, T), T)].astype(F32), back, 1
                )
                for n in range(3)
            ]
            left = jnp.where(lane < T - shift, tiles[0], tiles[1]).astype(BF)
            right = jnp.where(lane < T - shift, tiles[1], tiles[2])
            right = jnp.where(lane < RB - T, right, 0.0).astype(BF)
            if other == 0:
                OGR[kz, 0:TOK, 0:T] = left
                OGR[kz, 0:TOK, T : 2 * T] = right
            else:
                OGS[kz, :, 0:T] = left
                OGS[kz, :, T : 2 * T] = right
        return carry

    og_share = remote(OGS, OGR.at[:, pl.ds(TOK, TOK), :], cs.at[0], cr.at[0], sibling)
    at_share = remote(ATR.at[pl.ds(0, TOK), :], ATR.at[pl.ds(TOK, TOK), :], cs.at[1], cr.at[1], sibling)

    pieces = []
    for j in range(8):
        pos = (j // 2 % 2) * 9 + (j // 4) * 2 + j % 2
        pieces.append((pos * T, 208 * j, T))
        pieces.append((SHARE + 80 * j, 208 * j + T, 80))

    def order_columns(n, carry):
        size = 64
        block_rows = pl.ds(pl.multiple_of(n * size, size), size)
        lane = lanes(size)
        done = {}
        for dst, src, length in pieces:
            for t in range(dst // T, (dst + length - 1) // T + 1):
                for u in range(src // T, (src + length - 1) // T + 1):
                    low = max(dst, t * T, dst + T * u - src) - t * T
                    high = min(dst + length, (t + 1) * T, dst + T * (u + 1) - src) - t * T
                    if low >= high:
                        continue
                    tile = ATT[block_rows, u * T : (u + 1) * T].astype(F32)
                    shift = (dst - src) % T
                    if shift:
                        tile = pltpu.roll(tile, shift, 1)
                    if t in done:
                        tile = jnp.where((lane >= low) & (lane < high), tile, done[t])
                    done[t] = tile
        for t, tile in done.items():
            ATR[block_rows, t * T : (t + 1) * T] = tile.astype(BF)
        return carry

    def place(n):
        return (4 + ((n + 1) // 2) * (2 * (n % 2) - 1)) % 8

    def gy_copy(e, way):
        return remote(
            PG.at[zz(e), :, pl.ds(pl.multiple_of(take_col + 256 * way, T), 256)],
            YR.at[e, :, pl.ds(256 * way, 256)],
            gys.at[e, way], gyr.at[e, way], along_y(1 - 2 * way),
        )

    def partial_product(n, carry):
        e = place(n)
        for start, size in ((0, 512), (512, 640), (1152, 512)):
            prod = dot(OGR[zz(e), :, 0:RP], ATR[:, start : start + size], 0, 0)
            PG[zz(e), :, start : start + size] = prod.astype(BF)
        for way in (0, 1):
            gy_copy(e, way).start()
        return carry

    def gx_copy(e, half):
        turn = (half + jnp.minimum(e, 8 - e)) % 2
        return remote(
            PG.at[zz(e), rows(half), pl.ds(own_col, CARRY)],
            XR.at[e, rows(half), :],
            gxs.at[e, half], gxr.at[e, half], along_x(1 - 2 * turn),
        )

    def add_y(n, carry):
        e = place(n)
        for way in (0, 1):
            gy_copy(e, way).wait_recv()
        cols = pl.ds(give_col, SHARE)
        PG[zz(e), :, cols] = (PG[zz(e), :, cols].astype(F32) + YR[e].astype(F32)).astype(BF)

        @pl.when(is_b)
        def _():
            for half in (0, 1):
                gx_copy(e, half).start()

        return carry

    def add_x(n, carry):
        @pl.when(is_a)
        def _():
            e = place(n)
            for half in (0, 1):
                gx_copy(e, half).wait_recv()
            cols = pl.ds(own_col, CARRY)
            PG[zz(e), :, cols] = (PG[zz(e), :, cols].astype(F32) + XR[e].astype(F32)).astype(BF)

        return carry

    def gz_copy(way, half, reach):
        e = reach if way == 0 else 8 - reach
        return remote(
            PG.at[zz(e), rows(half), pl.ds(own_col, CARRY)],
            ZR.at[way, reach - 1, rows(half), :],
            gzs.at[way, half, reach - 1], gzr.at[way, half, reach - 1], along_z(1 - 2 * way),
        )

    def serve_gz(reach):
        @pl.when(is_a)
        def _():
            for half in (0, 1):
                for way in (0, 1):
                    top = chain(way, half)
                    if reach > top:
                        continue
                    if reach < top:
                        gz_copy(way, half, reach + 1).wait_recv()
                        e = (reach if way == 0 else 8 - reach) % 8
                        span = rows(half)
                        cols = pl.ds(own_col, CARRY)
                        PG[zz(e), span, cols] = (
                            PG[zz(e), span, cols].astype(F32) + ZR[way, reach, span, :].astype(F32)
                        ).astype(BF)
                    if reach > 0:
                        gz_copy(way, half, reach).start()

    turns = [(dy, dx) for dy in range(4) for dx in range(2)][1:]

    def owner(dy, dx):
        return (((y + dy) % 4) * 2 + (xh if dx == 0 else 1 - xh))

    def f_copy(dy, dx):
        slot = 2 * dy + dx
        size = 256 if dy % 2 == 0 else T
        return remote(
            LB.at[owner(dy, dx), :, pl.ds(0, size)],
            FR.at[slot, :, pl.ds(0, size)],
            fs.at[slot], fr.at[slot], owner_device(dy, dx),
        )

    def send_last():
        for j in range(8):
            u, shift = divmod(80 * j, T)
            tile = PG[z, :, SHARE + u * T : SHARE + (u + 1) * T].astype(F32)
            if shift:
                tile = pltpu.roll(tile, T - shift, 1)
            if shift + 80 > T:
                more = PG[z, :, SHARE + (u + 1) * T : SHARE + (u + 2) * T].astype(F32)
                tile = jnp.where(lanes(RP) < T - shift, tile, pltpu.roll(more, T - shift, 1))
            LB[j, :, 0:T] = tile.astype(BF)
        for m in range(4):
            j = (m // 2) * 4 + m % 2 + 2 * par
            LB[j, :, T : 2 * T] = PG[z, :, pl.ds(pl.multiple_of(par * CARRY + m * T, T), T)]
        for dy, dx in turns:
            f_copy(dy, dx).start()

    share = remote(SS, SR, cs.at[2], cr.at[2], sibling)

    def finish():
        me = owner(0, 0)
        rest = LB[me, :, 0:T].astype(F32)
        main = LB[me, :, T : 2 * T].astype(F32)
        for dy, dx in turns:
            f_copy(dy, dx).wait_recv()
            rest = rest + FR[2 * dy + dx, :, 0:T].astype(F32)
            if dy % 2 == 0:
                main = main + FR[2 * dy + dx, :, T : 2 * T].astype(F32)
        norm = 1.0 / math.sqrt(TOK * 256)
        main = main * norm
        rest = rest * norm
        second = jnp.where(lanes(RP) < 24, pltpu.roll(main, 24, 1), pltpu.roll(rest, 24, 1))
        SS[...] = jnp.where(c == 0, second, main)
        share.start()
        wg_ref[...] = jnp.where(c == 0, main, second)[0:RB, 0:104]

    def block(who, e):
        return mine(e) if who == 0 else theirs(e)

    def grad_in(who, group):
        for start, size in ((0, 512), (512, 640), (1152, 512)):
            cols = pl.ds(start, size)
            prods = [
                dot(OGR[zz(e), 0:TOK, 0:RP] if who == 0 else OGS[zz(e), :, 0:RP], W[block(who, e), :, cols], 1, 0)
                for e in group
            ]
            AGF[:, cols] += sum(prods[1:], prods[0])

    def project(who, group):
        att = ATT[...]
        lane = lanes(TOK)
        done = []
        for e in group:
            prod = dot(att, W[block(who, e)], 1, 1)
            shift = (RB * block(who, e)) % T
            one = pltpu.roll(prod[:, 0:T], shift, 1)
            tail = jnp.concatenate([prod[:, T:RP], jnp.zeros((TOK, 2 * T - RP), F32)], axis=1)
            two = pltpu.roll(tail, shift, 1)
            done.append((shift, one, two))
        for e, (shift, one, two) in zip(group, done):
            first = (RB * block(who, e)) // T

            def put(n, mask, value):
                cols = pl.ds(pl.multiple_of(jnp.minimum(first + n, D // T - 1) * T, T), T)
                old = LO[:, cols]
                new = (old.astype(F32) + value).astype(BF)
                LO[:, cols] = jnp.where(mask, new, old)

            put(0, lane >= shift, one)
            put(1, lane - shift < RB - T, jnp.where(lane < shift, one, two))
            put(2, lane < shift - (2 * T - RB), two)

    def backward(low, high):
        cols = [head_columns(h) for h in range(low, high)]
        qs, ks, vs, douts, atts = [[ref[:, col] for col in cols] for ref in (Q, K, V, AGB, ATT)]
        probs = [PST[h] for h in range(low, high)]
        deltas = [
            jnp.sum(dout.astype(F32) * att.astype(F32), axis=1, keepdims=True) for dout, att in zip(douts, atts)
        ]
        prob_grads = [dot(dout, v, 1, 1) for dout, v in zip(douts, vs)]
        grads = [(p * (g - delta)).astype(BF) for p, g, delta in zip(probs, prob_grads, deltas)]
        dvs = [dot(p.astype(BF), dout, 0, 0).astype(BF) for p, dout in zip(probs, douts)]
        dqs = [(dot(g, k, 1, 0) * factor).astype(BF) for g, k in zip(grads, ks)]
        dks = [(dot(g, q, 0, 0) * factor).astype(BF) for g, q in zip(grads, qs)]
        for n, col in enumerate(cols):
            Q[:, col] = dqs[n]
            K[:, col] = dks[n]
            V[:, col] = dvs[n]

    def loop(low, high, what):
        lax.fori_loop(low, high, what, 0)

    def serve_s(n):
        for e, half in chunks[n]:
            def go(e=e, half=half):
                for kind in (0, 1):
                    s_copy(e, half, kind, theirs).wait_recv()

            if e == 0:
                pl.when(is_a)(go)
            else:
                go()

    def zero_grad():
        AGF[...] = jnp.zeros((TOK, HD), F32)

    def round_grad():
        AGB[...] = AGF[...].astype(BF)

    def shares():
        og_share.wait()
        at_share.wait()

    does = {
        "load": lambda n: loads[n].wait(),
        "og": lambda a, b: loop(a, b, og_blocks),
        "ogs": og_share.start,
        "fwd": forward,
        "ord": lambda: loop(0, 4, order_columns),
        "ats": at_share.start,
        "shares": shares,
        "Z": serve_z, "X": serve_x, "S": serve_s,
        "YA": lambda n: serve_y(n, is_a),
        "YB": lambda n: serve_y(n, is_b),
        "part": lambda a, b: loop(a, b, partial_product),
        "ay": lambda a, b: loop(a, b, add_y),
        "ax": lambda a, b: loop(a, b, add_x),
        "gz": serve_gz,
        "zero": zero_grad,
        "E": lambda who, n: grad_in(who, GROUPS[n]),
        "G": lambda who, n: project(who, GROUPS[n]),
        "round": round_grad,
        "bwd": backward,
        "last": lambda: pl.when(is_a)(send_last),
        "fin": lambda: pl.when(is_a)(finish),
    }
    for name, *args in PLAN:
        does[name](*args)

    @pl.when(is_b)
    def _():
        share.wait_recv()
        wg_ref[...] = SR[0:RB, 0:104]

    for n in range(8):
        for e, half in chunks[n]:
            def sent(e=e, half=half):
                for way in (0, 1):
                    y_copy(e, half, way).wait_send()
                for kind in (0, 1):
                    s_copy(e, half, kind).wait_send()

            if e == 0:
                pl.when(is_b)(sent)
            else:
                sent()

    def sent_y(e, carry):
        for way in (0, 1):
            gy_copy(e, way).wait_send()
        return carry

    loop(0, 8, sent_y)

    @pl.when(is_b)
    def _():
        def sent_x(e, carry):
            for half in (0, 1):
                gx_copy(e, half).wait_send()
            return carry

        loop(0, 8, sent_x)
        for half in (0, 1):
            z_copy(half, half, 4).wait_send()

    @pl.when(is_a)
    def _():
        for e in (0, 1, 2, 3, 5, 6, 7):
            for half in (0, 1):
                x_copy(e, half).wait_send()
        for half in (0, 1):
            for way in (0, 1):
                for step in range(1, chain(way, half) + 1):
                    z_copy(way, half, step).wait_send()
                    gz_copy(way, half, step).wait_send()
        for dy, dx in turns:
            f_copy(dy, dx).wait_send()
        share.wait_send()


def store_kernel(*refs):
    sems = refs[-1]
    copies = [pltpu.make_async_copy(refs[n], refs[5 + n], sems.at[n]) for n in range(5)]
    for copy in copies:
        copy.start()
    for copy in copies:
        copy.wait()


def block_step(residual_in, queries, keys, values, segment_ids, weight_codes, weight_exponents, out_grad):
    vmem = pl.BlockSpec(memory_space=pltpu.VMEM)
    hbm = pl.BlockSpec(memory_space=pl.ANY)
    dma = pltpu.SemaphoreType.DMA
    V = pltpu.VMEM
    shapes = (((TOK, D), BF), ((TOK, HD), BF), ((TOK, HD), BF), ((TOK, HD), BF), ((RB, 104), F32))
    args = (segment_ids, weight_codes, weight_exponents.T, queries, keys, values, out_grad, residual_in)
    args = [pltpu.with_memory_space_constraint(arg, pltpu.HBM) for arg in args]
    outs = pl.pallas_call(
        body_kernel,
        out_shape=tuple(V(*shape) for shape in shapes),
        in_specs=[pl.BlockSpec(memory_space=pltpu.HBM)] * 8,
        out_specs=(vmem,) * 5,
        scratch_shapes=[
            V((16, RP, HD), BF),
            V((8, RP, HD), BF),
            V((8, RP, SHARE), BF),
            V((8, RP, CARRY), BF),
            V((2, 4, RP, CARRY), BF),
            V((8, RP, 2 * T), BF),
            V((8, RP, 2 * T), BF),
            V((RP, T), F32),
            V((RP, T), F32),
            V((8, 2 * TOK, 2 * T), BF),
            V((8, TOK, 2 * T), BF),
            V((2 * TOK, HD), BF),
            V((TOK, HD), BF),
            V((HEADS, TOK, TOK), F32),
            V((TOK, HD), F32),
            V((TOK, HD), BF),
            V((TOK, D), BF),
            V((TOK, TOK), F32),
            V((RB, HD), BF),
            V((HD // BLOCK, RB), jnp.int32),
            V((1, TOK), jnp.int32),
            dma((8,)),
            dma((2, 2, 4)), dma((2, 2, 4)),
            dma((8, 2)), dma((8, 2)),
            dma((8, 2, 2)), dma((8, 2, 2)),
            dma((8, 2, 2)), dma((8, 2, 2)),
            dma((8, 2)), dma((8, 2)),
            dma((8, 2)), dma((8, 2)),
            dma((2, 2, 4)), dma((2, 2, 4)),
            dma((8,)), dma((8,)),
            dma((3,)), dma((3,)),
        ],
        compiler_params=pltpu.CompilerParams(
            collective_id=0, has_side_effects=True, vmem_limit_bytes=48 * 2**20
        ),
        cost_estimate=pl.CostEstimate(flops=10**10, bytes_accessed=2 * 10**7, transcendentals=10**6),
    )(*args)
    outs = [pltpu.with_memory_space_constraint(out, pltpu.VMEM) for out in outs]
    return pl.pallas_call(
        store_kernel,
        out_shape=tuple(jax.ShapeDtypeStruct(*shape) for shape in shapes),
        in_specs=[hbm] * 5,
        out_specs=(hbm,) * 5,
        scratch_shapes=[dma((5,))],
        compiler_params=pltpu.CompilerParams(vmem_limit_bytes=2**20),
    )(*outs)


def solution(mesh):
    tokens = P(("outer", "inner"), None)
    in_specs = (tokens, tokens, tokens, tokens, tokens, P("inner", None), P("inner", None), tokens)
    out_specs = (tokens, tokens, tokens, tokens, P("inner", "outer"))
    return jax.shard_map(block_step, mesh=mesh, in_specs=in_specs, out_specs=out_specs, check_vma=False)
```

```python
import functools
import math

import jax
import jax.numpy as jnp
from jax import lax
from jax.experimental import pallas as pl
from jax.experimental.pallas import tpu as pltpu
from jax.sharding import PartitionSpec as P

MESH = pl.DeviceIdType.MESH
BF = jnp.bfloat16
F32 = jnp.float32

TOK = 256
D = 3200
HD = 1664
HEADS = 13
BLOCK = 32
T = 128
RB = 200
RP = 208
SPAN = ((0, 112), (112, 96))
CARRY = 1152
SHARE = 512
SPARE_X = True
TOP = (4, 3)

GROUPS = ((0,), (7, 1), (6, 2), (5, 3), (4,))

PLAN = (
    ("load", 6), ("load", 5), ("og", 0, 4), ("load", 4), ("og", 4, 8), ("load", 3), ("fwd", 0, 2), ("ogs",),
    ("fwd", 2, 4), ("fwd", 4, 6), ("fwd", 6, 8), ("fwd", 8, 10), ("fwd", 10, 12), ("Z", 1), ("fwd", 12, 13), ("ord",),
    ("ats",), ("X", 0), ("shares",), ("load", 7), ("part", 0, 1), ("X", 1), ("X", 2), ("Z", 2), ("Z", 3), ("YB", 0),
    ("YA", 1), ("YA", 2), ("ay", 0, 1), ("YA", 3), ("part", 1, 2), ("YB", 1), ("Z", 4), ("X", 3), ("zero",),
    ("ax", 0, 1), ("part", 2, 3), ("Z", 5), ("part", 3, 4), ("YB", 2), ("S", 0), ("gz", 4), ("ay", 1, 2), ("E", 0, 0),
    ("S", 1), ("S", 2), ("Z", 6), ("S", 3), ("ay", 2, 3), ("YB", 3), ("part", 4, 5), ("YA", 4), ("ax", 1, 2),
    ("part", 5, 6), ("ax", 2, 3), ("X", 4), ("G", 1, 0), ("gz", 3), ("X", 5), ("ay", 3, 4), ("ax", 3, 4), ("S", 4),
    ("Z", 7), ("part", 6, 7), ("YA", 5), ("ay", 4, 5), ("E", 1, 1), ("YA", 6), ("E", 0, 1), ("X", 6), ("ax", 4, 5),
    ("G", 0, 1), ("YB", 4), ("ay", 5, 6), ("gz", 2), ("part", 7, 8), ("G", 1, 2), ("ax", 5, 6), ("ay", 6, 7),
    ("S", 5), ("YB", 5), ("YB", 6), ("G", 0, 2), ("YA", 7), ("S", 6), ("ax", 6, 7), ("gz", 1), ("X", 7), ("ay", 7, 8),
    ("S", 7), ("G", 0, 3), ("YB", 7), ("E", 0, 4), ("ax", 7, 8), ("E", 0, 3), ("E", 1, 3), ("G", 1, 1), ("gz0", 0),
    ("last", 0), ("G", 0, 4), ("E", 1, 0), ("E", 1, 4), ("gz0", 1), ("last", 1), ("E", 0, 2), ("G", 1, 3),
    ("E", 1, 2), ("round",), ("bwd", 0, 2), ("bwd", 2, 4), ("G", 1, 4), ("bwd", 4, 6), ("bwd", 6, 8), ("bwd", 8, 10),
    ("G", 0, 0), ("fin",), ("bwd", 10, 12), ("bwd", 12, 13),
)


def chain(way, half):
    return TOP[half] if way == 0 else TOP[1 - half]


def dot(a, b, ca, cb):
    return lax.dot_general(a, b, (((ca,), (cb,)), ((), ())), preferred_element_type=F32)


def lanes(rows):
    return lax.broadcasted_iota(jnp.int32, (rows, T), 1)


def body_kernel(
    seg_hbm, codes_hbm, exps_hbm, q_hbm, k_hbm, v_hbm, og_hbm, res_hbm,
    LO, Q, K, V, wg_ref,
    W, PG, YR, XR, ZR, LB, FR, SR, SS, OGR, OGS, ATR, ATT, PST, AGF, AGB, OG, BIAS, CODES, EXPS, SEG,
    in_sem, zs, zr, xs, xr, ys, yr, ss, sr, gys, gyr, gxs, gxr, gzs, gzr, fs, fr, cs, cr,
):
    o = lax.axis_index("outer")
    i = lax.axis_index("inner")
    y = o // 4
    xh = (o // 2) % 2
    c = o % 2
    xl = i // 8
    z = i % 8
    x = xh * 2 + xl
    par = y % 2
    is_a = c == xl
    is_b = c != xl
    own_col = pl.multiple_of(par * SHARE, T)
    give_col = pl.multiple_of(par * CARRY, T)
    take_col = pl.multiple_of((1 - par) * CARRY, T)

    def device(x_, y_, z_, c_):
        return ((y_ * 2 + x_ // 2) * 2 + c_, (x_ % 2) * 8 + z_)

    def along_x(step):
        return device((x + step + 4) % 4, y, z, c)

    def along_y(step):
        return device(x, (y + step + 4) % 4, z, c)

    def along_z(step):
        return device(x, y, (z + step + 8) % 8, c)

    sibling = device(x, y, z, 1 - c)

    def owner_device(dy, dx):
        return device((xh if dx == 0 else 1 - xh) * 2 + xl, (y + dy) % 4, z, c)

    def remote(src, dst, ssem, rsem, dev):
        return pltpu.make_async_remote_copy(
            src_ref=src, dst_ref=dst, send_sem=ssem, recv_sem=rsem, device_id=dev, device_id_type=MESH
        )

    loads = [
        pltpu.make_async_copy(src, dst, in_sem.at[n])
        for n, (src, dst) in enumerate(
            ((codes_hbm, CODES), (exps_hbm, EXPS), (seg_hbm, SEG), (q_hbm, Q), (k_hbm, K), (v_hbm, V), (og_hbm, OG), (res_hbm, LO))
        )
    ]
    for load in loads[:3]:
        load.start()
    barrier = pltpu.get_barrier_semaphore()
    greet = [along_z(1), along_z(-1), along_x(1), along_x(-1), along_y(1), along_y(-1), sibling]
    greet += [owner_device(2, 0), owner_device(0, 1), owner_device(1, 1), owner_device(2, 1), owner_device(3, 1)]
    for dev in greet:
        pl.semaphore_signal(barrier, inc=1, device_id=dev, device_id_type=MESH)

    for load in loads[3:]:
        load.start()
    for load in loads[:3]:
        load.wait()
    exps = EXPS[...]
    scale = jnp.zeros(exps.shape, F32)
    for octave in range(-16, 1):
        scale = scale + jnp.where(exps == octave, 2.0**octave, 0.0)
    spread = (
        lax.broadcasted_iota(jnp.int32, (HD // BLOCK, HD), 1) // BLOCK
        == lax.broadcasted_iota(jnp.int32, (HD // BLOCK, HD), 0)
    ).astype(BF)
    wide = dot(scale.astype(BF), spread, 0, 0)
    block = CODES[...].astype(F32) * wide
    block = jnp.concatenate([block, jnp.zeros((RP - RB, HD), F32)], axis=0)
    W[xl * 8 + z] = block.astype(BF)

    pl.semaphore_wait(barrier, len(greet))

    def zz(e):
        return (z + e) % 8

    def rows(half):
        return pl.ds(*SPAN[half])

    def mine(e):
        return c * 8 + zz(e)

    def theirs(e):
        return (1 - c) * 8 + zz(e)

    def z_copy(way, half, step):
        e = (9 - step) % 8 if way == 0 else step - 1
        part = W.at[mine(e), rows(half), pl.ds(own_col, CARRY)]
        return remote(part, part, zs.at[way, half, step - 1], zr.at[way, half, step - 1], along_z(1 - 2 * way))

    def z_arrival(way, half, step):
        e = 8 - step if way == 0 else step
        part = W.at[mine(e), rows(half), pl.ds(own_col, CARRY)]
        return remote(part, part, zs.at[way, half, step - 1], zr.at[way, half, step - 1], along_z(1 - 2 * way))

    def x_copy(e, half):
        part = W.at[mine(e), rows(half), pl.ds(own_col, CARRY)]
        turn = (half + (e > 4)) % 2
        return remote(part, part, xs.at[e, half], xr.at[e, half], along_x(1 - 2 * turn))

    def y_copy(e, half, way):
        part = W.at[mine(e), rows(half), pl.ds(pl.multiple_of(give_col + 256 * way, T), 256)]
        return remote(part, part, ys.at[e, half, way], yr.at[e, half, way], along_y(1 - 2 * way))

    def y_arrival(e, half, way):
        part = W.at[mine(e), rows(half), pl.ds(pl.multiple_of(take_col + 256 * way, T), 256)]
        return remote(part, part, ys.at[e, half, way], yr.at[e, half, way], along_y(1 - 2 * way))

    def s_copy(e, half, kind, at=mine):
        cols = pl.ds(own_col, CARRY) if kind == 0 else pl.ds(take_col, SHARE)
        part = W.at[at(e), rows(half), cols]
        return remote(part, part, ss.at[e, half, kind], sr.at[e, half, kind], sibling)

    def spread_out(e, half):
        for way in (0, 1):
            y_copy(e, half, way).start()
        s_copy(e, half, 0).start()

    chunks = [
        [(0, 0), (0, 1)],
        [(7, 0), (1, 0)], [(7, 1), (1, 1)], [(6, 0), (2, 0)], [(6, 1), (2, 1)],
        [(5, 0), (3, 0)], [(5, 1), (3, 1)], [(4, 0), (4, 1)],
    ]

    def serve_z(n):
        @pl.when(is_a)
        def _():
            for e, half in chunks[n]:
                way = (0 if half == 0 else 1) if e == 4 else (0 if e > 4 else 1)
                step = 8 - e if way == 0 else e
                z_arrival(way, half, step).wait_recv()
                if step < chain(way, half):
                    z_copy(way, half, step + 1).start()
                if e != 4:
                    x_copy(e, half).start()
                spread_out(e, half)

    def serve_x(n):
        @pl.when(is_b)
        def _():
            for e, half in chunks[n]:
                if e == 4:
                    z_arrival(half, half, 4).wait_recv()
                else:
                    x_copy(e, half).wait_recv()
                if (e, half) in ((5, 0), (3, 1)):
                    z_copy(half, half, 4).start()
                spread_out(e, half)

    def serve_y(n, role):
        @pl.when(role)
        def _():
            for e, half in chunks[n]:
                for way in (0, 1):
                    y_arrival(e, half, way).wait_recv()
                s_copy(e, half, 1).start()

    @pl.when(is_a)
    def _():
        for half in (0, 1):
            for way in (0, 1):
                z_copy(way, half, 1).start()
            x_copy(0, half).start()

    seg = jnp.broadcast_to(SEG[...].astype(F32), (TOK, TOK))
    BIAS[...] = jnp.where(seg == seg.T, 0.0, -1e30)
    factor = 1.0 / math.sqrt(T)

    def head_columns(h):
        return slice(h * T, (h + 1) * T)

    def forward(low, high):
        cols = [head_columns(h) for h in range(low, high)]
        qs, ks, vs = [[ref[:, col] for col in cols] for ref in (Q, K, V)]
        bias = BIAS[...]
        scores = [dot(q, k, 1, 1) * factor + bias for q, k in zip(qs, ks)]
        tops = [jnp.max(s, axis=1, keepdims=True) for s in scores]
        scores = [jnp.exp(s - top) for s, top in zip(scores, tops)]
        sums = [1.0 / jnp.sum(s, axis=1, keepdims=True) for s in scores]
        probs = [s * inverse for s, inverse in zip(scores, sums)]
        outs = [dot(p.astype(BF), v, 1, 0).astype(BF) for p, v in zip(probs, vs)]
        for n, h in enumerate(range(low, high)):
            PST[h] = probs[n]
            ATT[:, cols[n]] = outs[n]

    def og_blocks(kz, carry):
        lane = lanes(TOK)
        for other in (0, 1):
            b = (c if other == 0 else 1 - c) * 8 + kz
            first = (RB * b) // T
            shift = (RB * b) % T
            back = (T - shift) % T
            tiles = [
                pltpu.roll(
                    OG[:, pl.ds(pl.multiple_of(jnp.minimum(first + n, D // T - 1) * T, T), T)].astype(F32), back, 1
                )
                for n in range(3)
            ]
            left = jnp.where(lane < T - shift, tiles[0], tiles[1]).astype(BF)
            right = jnp.where(lane < T - shift, tiles[1], tiles[2])
            right = jnp.where(lane < RB - T, right, 0.0).astype(BF)
            if other == 0:
                OGR[kz, 0:TOK, 0:T] = left
                OGR[kz, 0:TOK, T : 2 * T] = right
            else:
                OGS[kz, :, 0:T] = left
                OGS[kz, :, T : 2 * T] = right
        return carry

    og_share = remote(OGS, OGR.at[:, pl.ds(TOK, TOK), :], cs.at[0], cr.at[0], sibling)
    at_share = remote(ATR.at[pl.ds(0, TOK), :], ATR.at[pl.ds(TOK, TOK), :], cs.at[1], cr.at[1], sibling)

    pieces = []
    for j in range(8):
        pos = (j // 2 % 2) * 9 + (j // 4) * 2 + j % 2
        pieces.append((pos * T, 208 * j, T))
        pieces.append((SHARE + 80 * j, 208 * j + T, 80))

    def order_columns(n, carry):
        size = 64
        block_rows = pl.ds(pl.multiple_of(n * size, size), size)
        lane = lanes(size)
        done = {}
        for dst, src, length in pieces:
            for t in range(dst // T, (dst + length - 1) // T + 1):
                for u in range(src // T, (src + length - 1) // T + 1):
                    low = max(dst, t * T, dst + T * u - src) - t * T
                    high = min(dst + length, (t + 1) * T, dst + T * (u + 1) - src) - t * T
                    if low >= high:
                        continue
                    tile = ATT[block_rows, u * T : (u + 1) * T].astype(F32)
                    shift = (dst - src) % T
                    if shift:
                        tile = pltpu.roll(tile, shift, 1)
                    if t in done:
                        tile = jnp.where((lane >= low) & (lane < high), tile, done[t])
                    done[t] = tile
        for t, tile in done.items():
            ATR[block_rows, t * T : (t + 1) * T] = tile.astype(BF)
        return carry

    def place(n):
        return (4 + ((n + 1) // 2) * (2 * (n % 2) - 1)) % 8

    def gy_copy(e, way):
        return remote(
            PG.at[zz(e), :, pl.ds(pl.multiple_of(take_col + 256 * way, T), 256)],
            YR.at[e, :, pl.ds(256 * way, 256)],
            gys.at[e, way], gyr.at[e, way], along_y(1 - 2 * way),
        )

    def partial_product(n, carry):
        e = place(n)
        for start, size in ((0, 512), (512, 640), (1152, 512)):
            prod = dot(OGR[zz(e), :, 0:RP], ATR[:, start : start + size], 0, 0)
            PG[zz(e), :, start : start + size] = prod.astype(BF)
        for way in (0, 1):
            gy_copy(e, way).start()
        return carry

    def gx_copy(e, half):
        turn = (half + min(e, 8 - e)) % 2
        return remote(
            PG.at[zz(e), rows(half), pl.ds(own_col, CARRY)],
            XR.at[e, rows(half), :],
            gxs.at[e, half], gxr.at[e, half], along_x(1 - 2 * turn),
        )

    def add_y(low):
        e = place(low)
        for way in (0, 1):
            gy_copy(e, way).wait_recv()
        cols = pl.ds(give_col, SHARE)
        PG[zz(e), :, cols] = (PG[zz(e), :, cols].astype(F32) + YR[e].astype(F32)).astype(BF)

        @pl.when(is_b)
        def _():
            if not SPARE_X:
                send = True
            elif low == 0:
                send = False
                for half in (0, 1):
                    gz_copy(half, half, 4).start()
            else:
                send = True
                if low in (1, 2):
                    half = 2 - low
                    gz_copy(half, half, 4).wait_recv()
                    span = rows(half)
                    mid = pl.ds(own_col, CARRY)
                    PG[zz(e), span, mid] = (
                        PG[zz(e), span, mid].astype(F32) + ZR[half, 3, span, :].astype(F32)
                    ).astype(BF)
            if send:
                for half in (0, 1):
                    gx_copy(e, half).start()

    def add_x(n):
        if SPARE_X and n == 0:
            return

        @pl.when(is_a)
        def _():
            e = place(n)
            for half in (0, 1):
                gx_copy(e, half).wait_recv()
            cols = pl.ds(own_col, CARRY)
            PG[zz(e), :, cols] = (PG[zz(e), :, cols].astype(F32) + XR[e].astype(F32)).astype(BF)

    def gz_copy(way, half, reach):
        e = reach if way == 0 else 8 - reach
        return remote(
            PG.at[zz(e), rows(half), pl.ds(own_col, CARRY)],
            ZR.at[way, reach - 1, rows(half), :],
            gzs.at[way, half, reach - 1], gzr.at[way, half, reach - 1], along_z(1 - 2 * way),
        )

    def serve_gz(reach, halves=(0, 1)):
        @pl.when(is_a)
        def _():
            for half in halves:
                for way in (0, 1):
                    top = chain(way, half)
                    if reach > top:
                        continue
                    if reach < top:
                        gz_copy(way, half, reach + 1).wait_recv()
                        e = (reach if way == 0 else 8 - reach) % 8
                        span = rows(half)
                        cols = pl.ds(own_col, CARRY)
                        PG[zz(e), span, cols] = (
                            PG[zz(e), span, cols].astype(F32) + ZR[way, reach, span, :].astype(F32)
                        ).astype(BF)
                    if reach > 0:
                        gz_copy(way, half, reach).start()

    turns = [(dy, dx) for dy in range(4) for dx in range(2)][1:]

    def owner(dy, dx):
        return (((y + dy) % 4) * 2 + (xh if dx == 0 else 1 - xh))

    def f_copy(dy, dx, half):
        slot = 2 * dy + dx
        size = 256 if dy % 2 == 0 else T
        return remote(
            LB.at[owner(dy, dx), rows(half), pl.ds(0, size)],
            FR.at[slot, rows(half), pl.ds(0, size)],
            fs.at[slot, half], fr.at[slot, half], owner_device(dy, dx),
        )

    def send_last(half):
        span = rows(half)
        for j in range(8):
            u, shift = divmod(80 * j, T)
            tile = PG[z, span, SHARE + u * T : SHARE + (u + 1) * T].astype(F32)
            if shift:
                tile = pltpu.roll(tile, T - shift, 1)
            if shift + 80 > T:
                more = PG[z, span, SHARE + (u + 1) * T : SHARE + (u + 2) * T].astype(F32)
                tile = jnp.where(lanes(SPAN[half][1]) < T - shift, tile, pltpu.roll(more, T - shift, 1))
            LB[j, span, 0:T] = tile.astype(BF)
        for m in range(4):
            j = (m // 2) * 4 + m % 2 + 2 * par
            LB[j, span, T : 2 * T] = PG[z, span, pl.ds(pl.multiple_of(par * CARRY + m * T, T), T)]
        for dy, dx in turns:
            f_copy(dy, dx, half).start()

    share = remote(SS, SR, cs.at[2], cr.at[2], sibling)

    def finish():
        me = owner(0, 0)
        rest = LB[me, :, 0:T].astype(F32)
        main = LB[me, :, T : 2 * T].astype(F32)
        for dy, dx in turns:
            for half in (0, 1):
                f_copy(dy, dx, half).wait_recv()
            rest = rest + FR[2 * dy + dx, :, 0:T].astype(F32)
            if dy % 2 == 0:
                main = main + FR[2 * dy + dx, :, T : 2 * T].astype(F32)
        norm = 1.0 / math.sqrt(TOK * 256)
        main = main * norm
        rest = rest * norm
        second = jnp.where(lanes(RP) < 24, pltpu.roll(main, 24, 1), pltpu.roll(rest, 24, 1))
        SS[...] = jnp.where(c == 0, second, main)
        share.start()
        wg_ref[...] = jnp.where(c == 0, main, second)[0:RB, 0:104]

    def block(who, e):
        return mine(e) if who == 0 else theirs(e)

    def grad_in(who, group):
        for start, size in ((0, 512), (512, 640), (1152, 512)):
            cols = pl.ds(start, size)
            prods = [
                dot(OGR[zz(e), 0:TOK, 0:RP] if who == 0 else OGS[zz(e), :, 0:RP], W[block(who, e), :, cols], 1, 0)
                for e in group
            ]
            AGF[:, cols] += sum(prods[1:], prods[0])

    def project(who, group):
        att = ATT[...]
        lane = lanes(TOK)
        done = []
        for e in group:
            prod = dot(att, W[block(who, e)], 1, 1)
            shift = (RB * block(who, e)) % T
            one = pltpu.roll(prod[:, 0:T], shift, 1)
            tail = jnp.concatenate([prod[:, T:RP], jnp.zeros((TOK, 2 * T - RP), F32)], axis=1)
            two = pltpu.roll(tail, shift, 1)
            done.append((shift, one, two))
        for e, (shift, one, two) in zip(group, done):
            first = (RB * block(who, e)) // T

            def put(n, mask, value):
                cols = pl.ds(pl.multiple_of(jnp.minimum(first + n, D // T - 1) * T, T), T)
                old = LO[:, cols]
                new = (old.astype(F32) + value).astype(BF)
                LO[:, cols] = jnp.where(mask, new, old)

            put(0, lane >= shift, one)
            put(1, lane - shift < RB - T, jnp.where(lane < shift, one, two))
            put(2, lane < shift - (2 * T - RB), two)

    def backward(low, high):
        cols = [head_columns(h) for h in range(low, high)]
        qs, ks, vs, douts, atts = [[ref[:, col] for col in cols] for ref in (Q, K, V, AGB, ATT)]
        probs = [PST[h] for h in range(low, high)]
        deltas = [
            jnp.sum(dout.astype(F32) * att.astype(F32), axis=1, keepdims=True) for dout, att in zip(douts, atts)
        ]
        prob_grads = [dot(dout, v, 1, 1) for dout, v in zip(douts, vs)]
        grads = [(p * (g - delta)).astype(BF) for p, g, delta in zip(probs, prob_grads, deltas)]
        dvs = [dot(p.astype(BF), dout, 0, 0).astype(BF) for p, dout in zip(probs, douts)]
        dqs = [(dot(g, k, 1, 0) * factor).astype(BF) for g, k in zip(grads, ks)]
        dks = [(dot(g, q, 0, 0) * factor).astype(BF) for g, q in zip(grads, qs)]
        for n, col in enumerate(cols):
            Q[:, col] = dqs[n]
            K[:, col] = dks[n]
            V[:, col] = dvs[n]

    def loop(low, high, what):
        lax.fori_loop(low, high, what, 0)

    def serve_s(n):
        for e, half in chunks[n]:
            def go(e=e, half=half):
                for kind in (0, 1):
                    s_copy(e, half, kind, theirs).wait_recv()

            if e == 0:
                pl.when(is_a)(go)
            else:
                go()

    def zero_grad():
        AGF[...] = jnp.zeros((TOK, HD), F32)

    def round_grad():
        AGB[...] = AGF[...].astype(BF)

    def shares():
        og_share.wait()
        at_share.wait()

    does = {
        "load": lambda n: loads[n].wait(),
        "og": lambda a, b: loop(a, b, og_blocks),
        "ogs": og_share.start,
        "fwd": forward,
        "ord": lambda: loop(0, 4, order_columns),
        "ats": at_share.start,
        "shares": shares,
        "Z": serve_z, "X": serve_x, "S": serve_s,
        "YA": lambda n: serve_y(n, is_a),
        "YB": lambda n: serve_y(n, is_b),
        "part": lambda a, b: loop(a, b, partial_product),
        "ay": lambda a, b: add_y(a),
        "ax": lambda a, b: add_x(a),
        "gz": serve_gz,
        "zero": zero_grad,
        "E": lambda who, n: grad_in(who, GROUPS[n]),
        "G": lambda who, n: project(who, GROUPS[n]),
        "round": round_grad,
        "bwd": backward,
        "gz0": lambda half: serve_gz(0, (half,)),
        "last": lambda half: pl.when(is_a)(functools.partial(send_last, half)),
        "fin": lambda: pl.when(is_a)(finish),
    }
    for name, *args in PLAN:
        does[name](*args)

    @pl.when(is_b)
    def _():
        share.wait_recv()
        wg_ref[...] = SR[0:RB, 0:104]

    for n in range(8):
        for e, half in chunks[n]:
            def sent(e=e, half=half):
                for way in (0, 1):
                    y_copy(e, half, way).wait_send()
                for kind in (0, 1):
                    s_copy(e, half, kind).wait_send()

            if e == 0:
                pl.when(is_b)(sent)
            else:
                sent()

    def sent_y(e, carry):
        for way in (0, 1):
            gy_copy(e, way).wait_send()
        return carry

    loop(0, 8, sent_y)

    @pl.when(is_b)
    def _():
        for e in range(8):
            if SPARE_X and e == 4:
                continue
            for half in (0, 1):
                gx_copy(e, half).wait_send()
        for half in (0, 1):
            z_copy(half, half, 4).wait_send()
            if SPARE_X:
                gz_copy(half, half, 4).wait_send()

    @pl.when(is_a)
    def _():
        for e in (0, 1, 2, 3, 5, 6, 7):
            for half in (0, 1):
                x_copy(e, half).wait_send()
        for half in (0, 1):
            for way in (0, 1):
                for step in range(1, chain(way, half) + 1):
                    z_copy(way, half, step).wait_send()
                    gz_copy(way, half, step).wait_send()
        for dy, dx in turns:
            for half in (0, 1):
                f_copy(dy, dx, half).wait_send()
        share.wait_send()


def store_kernel(*refs):
    sems = refs[-1]
    copies = [pltpu.make_async_copy(refs[n], refs[5 + n], sems.at[n]) for n in range(5)]
    for copy in copies:
        copy.start()
    for copy in copies:
        copy.wait()


def block_step(residual_in, queries, keys, values, segment_ids, weight_codes, weight_exponents, out_grad):
    vmem = pl.BlockSpec(memory_space=pltpu.VMEM)
    hbm = pl.BlockSpec(memory_space=pl.ANY)
    dma = pltpu.SemaphoreType.DMA
    V = pltpu.VMEM
    shapes = (((TOK, D), BF), ((TOK, HD), BF), ((TOK, HD), BF), ((TOK, HD), BF), ((RB, 104), F32))
    args = (segment_ids, weight_codes, weight_exponents.T, queries, keys, values, out_grad, residual_in)
    args = [pltpu.with_memory_space_constraint(arg, pltpu.HBM) for arg in args]
    outs = pl.pallas_call(
        body_kernel,
        out_shape=tuple(V(*shape) for shape in shapes),
        in_specs=[pl.BlockSpec(memory_space=pltpu.HBM)] * 8,
        out_specs=(vmem,) * 5,
        scratch_shapes=[
            V((16, RP, HD), BF),
            V((8, RP, HD), BF),
            V((8, RP, SHARE), BF),
            V((8, RP, CARRY), BF),
            V((2, 4, RP, CARRY), BF),
            V((8, RP, 2 * T), BF),
            V((8, RP, 2 * T), BF),
            V((RP, T), F32),
            V((RP, T), F32),
            V((8, 2 * TOK, 2 * T), BF),
            V((8, TOK, 2 * T), BF),
            V((2 * TOK, HD), BF),
            V((TOK, HD), BF),
            V((HEADS, TOK, TOK), F32),
            V((TOK, HD), F32),
            V((TOK, HD), BF),
            V((TOK, D), BF),
            V((TOK, TOK), F32),
            V((RB, HD), BF),
            V((HD // BLOCK, RB), jnp.int32),
            V((1, TOK), jnp.int32),
            dma((8,)),
            dma((2, 2, 4)), dma((2, 2, 4)),
            dma((8, 2)), dma((8, 2)),
            dma((8, 2, 2)), dma((8, 2, 2)),
            dma((8, 2, 2)), dma((8, 2, 2)),
            dma((8, 2)), dma((8, 2)),
            dma((8, 2)), dma((8, 2)),
            dma((2, 2, 4)), dma((2, 2, 4)),
            dma((8, 2)), dma((8, 2)),
            dma((3,)), dma((3,)),
        ],
        compiler_params=pltpu.CompilerParams(
            collective_id=0, has_side_effects=True, vmem_limit_bytes=48 * 2**20
        ),
        cost_estimate=pl.CostEstimate(flops=10**10, bytes_accessed=2 * 10**7, transcendentals=10**6),
    )(*args)
    outs = [pltpu.with_memory_space_constraint(out, pltpu.VMEM) for out in outs]
    return pl.pallas_call(
        store_kernel,
        out_shape=tuple(jax.ShapeDtypeStruct(*shape) for shape in shapes),
        in_specs=[hbm] * 5,
        out_specs=(hbm,) * 5,
        scratch_shapes=[dma((5,))],
        compiler_params=pltpu.CompilerParams(vmem_limit_bytes=2**20),
    )(*outs)


def solution(mesh):
    tokens = P(("outer", "inner"), None)
    in_specs = (tokens, tokens, tokens, tokens, tokens, P("inner", None), P("inner", None), tokens)
    out_specs = (tokens, tokens, tokens, tokens, P("inner", "outer"))
    return jax.shard_map(block_step, mesh=mesh, in_specs=in_specs, out_specs=out_specs, check_vma=False)
```

```python
import functools
import math

import jax
import jax.numpy as jnp
from jax import lax
from jax.experimental import pallas as pl
from jax.experimental.pallas import tpu as pltpu
from jax.sharding import PartitionSpec as P

MESH = pl.DeviceIdType.MESH
BF = jnp.bfloat16
F32 = jnp.float32

TOK = 256
D = 3200
HD = 1664
HEADS = 13
BLOCK = 32
T = 128
RB = 200
RP = 208
SPAN = ((0, 112), (112, 96))
CARRY = 1152
SHARE = 512
SPARE_X = True
TOP = (4, 3)

GROUPS = ((0,), (7, 1), (6, 2), (5, 3), (4,))

PLAN = (
    ("load", 6), ("load", 5), ("load", 4), ("load", 3), ("og", 0, 4), ("fwd", 0, 2), ("og", 4, 8), ("fwd", 2, 4),
    ("fwd", 4, 6), ("fwd", 6, 8), ("load", 7), ("fwd", 8, 10), ("ogs",), ("fwd", 10, 12), ("fwd", 12, 13), ("ord",),
    ("ats",), ("Z", 1), ("X", 0), ("Z", 2), ("shares",), ("YB", 0), ("part", 0, 1), ("X", 1), ("part", 1, 2),
    ("Z", 3), ("part", 2, 3), ("Z", 4), ("ay", 0, 1), ("YA", 1), ("part", 3, 4), ("Z", 5), ("part", 4, 5),
    ("ax", 0, 1), ("YA", 2), ("X", 2), ("Z", 6), ("YA", 3), ("part", 5, 6), ("zero",), ("S", 0), ("gz", 4),
    ("ay", 1, 2), ("part", 6, 7), ("ay", 2, 3), ("X", 3), ("E", 0, 0), ("X", 4), ("ax", 1, 2), ("ay", 3, 4),
    ("YB", 1), ("part", 7, 8), ("X", 5), ("YA", 4), ("X", 6), ("ax", 2, 3), ("gz", 3), ("ax", 3, 4), ("ay", 4, 5),
    ("S", 1), ("ax", 4, 5), ("gz", 2), ("ay", 5, 6), ("S", 2), ("ay", 6, 7), ("YB", 2), ("Z", 7), ("G", 1, 0),
    ("YB", 3), ("S", 3), ("ax", 5, 6), ("E", 1, 0), ("ax", 6, 7), ("gz", 1), ("X", 7), ("YB", 4), ("ay", 7, 8),
    ("G", 0, 1), ("YA", 5), ("ax", 7, 8), ("E", 0, 2), ("YB", 5), ("S", 4), ("YA", 6), ("G", 0, 0), ("YB", 6),
    ("gz0", 0), ("YB", 7), ("YA", 7), ("E", 0, 3), ("S", 5), ("last", 0), ("G", 0, 3), ("G", 1, 1), ("E", 0, 4),
    ("gz0", 1), ("S", 6), ("last", 1), ("S", 7), ("E", 1, 3), ("E", 1, 1), ("E", 0, 1), ("E", 1, 2), ("G", 0, 4),
    ("G", 0, 2), ("G", 1, 2), ("E", 1, 4), ("round",), ("bwd", 0, 2), ("bwd", 2, 4), ("bwd", 4, 6), ("G", 1, 4),
    ("bwd", 6, 8), ("fin",), ("G", 1, 3), ("bwd", 8, 10), ("bwd", 10, 12), ("bwd", 12, 13),
)


def chain(way, half):
    return TOP[half] if way == 0 else TOP[1 - half]


def dot(a, b, ca, cb):
    return lax.dot_general(a, b, (((ca,), (cb,)), ((), ())), preferred_element_type=F32)


def lanes(rows):
    return lax.broadcasted_iota(jnp.int32, (rows, T), 1)


def body_kernel(
    seg_hbm, codes_hbm, exps_hbm, q_hbm, k_hbm, v_hbm, og_hbm, res_hbm,
    LO, Q, K, V, wg_ref,
    W, PG, YR, XR, ZR, LB, FR, SR, SS, OGR, OGS, ATR, ATT, PST, AGF, AGB, OG, BIAS, CODES, EXPS, SEG,
    in_sem, zs, zr, xs, xr, ys, yr, ss, sr, gys, gyr, gxs, gxr, gzs, gzr, fs, fr, cs, cr,
):
    o = lax.axis_index("outer")
    i = lax.axis_index("inner")
    y = o // 4
    xh = (o // 2) % 2
    c = o % 2
    xl = i // 8
    z = i % 8
    x = xh * 2 + xl
    par = y % 2
    is_a = c == xl
    is_b = c != xl
    own_col = pl.multiple_of(par * SHARE, T)
    give_col = pl.multiple_of(par * CARRY, T)
    take_col = pl.multiple_of((1 - par) * CARRY, T)

    def device(x_, y_, z_, c_):
        return ((y_ * 2 + x_ // 2) * 2 + c_, (x_ % 2) * 8 + z_)

    def along_x(step):
        return device((x + step + 4) % 4, y, z, c)

    def along_y(step):
        return device(x, (y + step + 4) % 4, z, c)

    def along_z(step):
        return device(x, y, (z + step + 8) % 8, c)

    sibling = device(x, y, z, 1 - c)

    def owner_device(dy, dx):
        return device((xh if dx == 0 else 1 - xh) * 2 + xl, (y + dy) % 4, z, c)

    def remote(src, dst, ssem, rsem, dev):
        return pltpu.make_async_remote_copy(
            src_ref=src, dst_ref=dst, send_sem=ssem, recv_sem=rsem, device_id=dev, device_id_type=MESH
        )

    loads = [
        pltpu.make_async_copy(src, dst, in_sem.at[n])
        for n, (src, dst) in enumerate(
            ((codes_hbm, CODES), (exps_hbm, EXPS), (seg_hbm, SEG), (q_hbm, Q), (k_hbm, K), (v_hbm, V), (og_hbm, OG), (res_hbm, LO))
        )
    ]
    for load in loads[:3]:
        load.start()
    barrier = pltpu.get_barrier_semaphore()
    greet = [along_z(1), along_z(-1), along_x(1), along_x(-1), along_y(1), along_y(-1), sibling]
    greet += [owner_device(2, 0), owner_device(0, 1), owner_device(1, 1), owner_device(2, 1), owner_device(3, 1)]
    for dev in greet:
        pl.semaphore_signal(barrier, inc=1, device_id=dev, device_id_type=MESH)

    for load in loads[3:]:
        load.start()
    for load in loads[:3]:
        load.wait()
    exps = EXPS[...]
    scale = jnp.zeros(exps.shape, F32)
    for octave in range(-16, 1):
        scale = scale + jnp.where(exps == octave, 2.0**octave, 0.0)
    spread = (
        lax.broadcasted_iota(jnp.int32, (HD // BLOCK, HD), 1) // BLOCK
        == lax.broadcasted_iota(jnp.int32, (HD // BLOCK, HD), 0)
    ).astype(BF)
    wide = dot(scale.astype(BF), spread, 0, 0)
    block = CODES[...].astype(F32) * wide
    block = jnp.concatenate([block, jnp.zeros((RP - RB, HD), F32)], axis=0)
    W[xl * 8 + z] = block.astype(BF)

    pl.semaphore_wait(barrier, len(greet))

    def zz(e):
        return (z + e) % 8

    def rows(half):
        return pl.ds(*SPAN[half])

    def mine(e):
        return c * 8 + zz(e)

    def theirs(e):
        return (1 - c) * 8 + zz(e)

    def z_copy(way, half, step):
        e = (9 - step) % 8 if way == 0 else step - 1
        part = W.at[mine(e), rows(half), pl.ds(own_col, CARRY)]
        return remote(part, part, zs.at[way, half, step - 1], zr.at[way, half, step - 1], along_z(1 - 2 * way))

    def z_arrival(way, half, step):
        e = 8 - step if way == 0 else step
        part = W.at[mine(e), rows(half), pl.ds(own_col, CARRY)]
        return remote(part, part, zs.at[way, half, step - 1], zr.at[way, half, step - 1], along_z(1 - 2 * way))

    def x_copy(e, half):
        part = W.at[mine(e), rows(half), pl.ds(own_col, CARRY)]
        turn = (half + (e > 4)) % 2
        return remote(part, part, xs.at[e, half], xr.at[e, half], along_x(1 - 2 * turn))

    def y_copy(e, half, way):
        part = W.at[mine(e), rows(half), pl.ds(pl.multiple_of(give_col + 256 * way, T), 256)]
        return remote(part, part, ys.at[e, half, way], yr.at[e, half, way], along_y(1 - 2 * way))

    def y_arrival(e, half, way):
        part = W.at[mine(e), rows(half), pl.ds(pl.multiple_of(take_col + 256 * way, T), 256)]
        return remote(part, part, ys.at[e, half, way], yr.at[e, half, way], along_y(1 - 2 * way))

    def s_copy(e, half, kind, at=mine):
        cols = pl.ds(own_col, CARRY) if kind == 0 else pl.ds(take_col, SHARE)
        part = W.at[at(e), rows(half), cols]
        return remote(part, part, ss.at[e, half, kind], sr.at[e, half, kind], sibling)

    def spread_out(e, half):
        for way in (0, 1):
            y_copy(e, half, way).start()
        s_copy(e, half, 0).start()

    chunks = [
        [(0, 0), (0, 1)],
        [(7, 0), (1, 0)], [(7, 1), (1, 1)], [(6, 0), (2, 0)], [(6, 1), (2, 1)],
        [(5, 0), (3, 0)], [(5, 1), (3, 1)], [(4, 0), (4, 1)],
    ]

    def serve_z(n):
        @pl.when(is_a)
        def _():
            for e, half in chunks[n]:
                way = (0 if half == 0 else 1) if e == 4 else (0 if e > 4 else 1)
                step = 8 - e if way == 0 else e
                z_arrival(way, half, step).wait_recv()
                if step < chain(way, half):
                    z_copy(way, half, step + 1).start()
                if e != 4:
                    x_copy(e, half).start()
                spread_out(e, half)

    def serve_x(n):
        @pl.when(is_b)
        def _():
            for e, half in chunks[n]:
                if e == 4:
                    z_arrival(half, half, 4).wait_recv()
                else:
                    x_copy(e, half).wait_recv()
                if (e, half) in ((5, 0), (3, 1)):
                    z_copy(half, half, 4).start()
                spread_out(e, half)

    def serve_y(n, role):
        @pl.when(role)
        def _():
            for e, half in chunks[n]:
                for way in (0, 1):
                    y_arrival(e, half, way).wait_recv()
                s_copy(e, half, 1).start()

    @pl.when(is_a)
    def _():
        for half in (0, 1):
            for way in (0, 1):
                z_copy(way, half, 1).start()
            x_copy(0, half).start()

    seg = jnp.broadcast_to(SEG[...].astype(F32), (TOK, TOK))
    BIAS[...] = jnp.where(seg == seg.T, 0.0, -1e30)
    factor = 1.0 / math.sqrt(T)

    def head_columns(h):
        return slice(h * T, (h + 1) * T)

    def forward(low, high):
        cols = [head_columns(h) for h in range(low, high)]
        qs, ks, vs = [[ref[:, col] for col in cols] for ref in (Q, K, V)]
        bias = BIAS[...]
        scores = [dot(q, k, 1, 1) * factor + bias for q, k in zip(qs, ks)]
        tops = [jnp.max(s, axis=1, keepdims=True) for s in scores]
        scores = [jnp.exp(s - top) for s, top in zip(scores, tops)]
        sums = [1.0 / jnp.sum(s, axis=1, keepdims=True) for s in scores]
        probs = [s * inverse for s, inverse in zip(scores, sums)]
        outs = [dot(p.astype(BF), v, 1, 0).astype(BF) for p, v in zip(probs, vs)]
        for n, h in enumerate(range(low, high)):
            PST[h] = probs[n]
            ATT[:, cols[n]] = outs[n]

    def og_blocks(kz, carry):
        lane = lanes(TOK)
        for other in (0, 1):
            b = (c if other == 0 else 1 - c) * 8 + kz
            first = (RB * b) // T
            shift = (RB * b) % T
            back = (T - shift) % T
            tiles = [
                pltpu.roll(
                    OG[:, pl.ds(pl.multiple_of(jnp.minimum(first + n, D // T - 1) * T, T), T)].astype(F32), back, 1
                )
                for n in range(3)
            ]
            left = jnp.where(lane < T - shift, tiles[0], tiles[1]).astype(BF)
            right = jnp.where(lane < T - shift, tiles[1], tiles[2])
            right = jnp.where(lane < RB - T, right, 0.0).astype(BF)
            if other == 0:
                OGR[kz, 0:TOK, 0:T] = left
                OGR[kz, 0:TOK, T : 2 * T] = right
            else:
                OGS[kz, :, 0:T] = left
                OGS[kz, :, T : 2 * T] = right
        return carry

    og_share = remote(OGS, OGR.at[:, pl.ds(TOK, TOK), :], cs.at[0], cr.at[0], sibling)
    at_share = remote(ATR.at[pl.ds(0, TOK), :], ATR.at[pl.ds(TOK, TOK), :], cs.at[1], cr.at[1], sibling)

    pieces = []
    for j in range(8):
        pos = (j // 2 % 2) * 9 + (j // 4) * 2 + j % 2
        pieces.append((pos * T, 208 * j, T))
        pieces.append((SHARE + 80 * j, 208 * j + T, 80))

    def order_columns(n, carry):
        size = 64
        block_rows = pl.ds(pl.multiple_of(n * size, size), size)
        lane = lanes(size)
        done = {}
        for dst, src, length in pieces:
            for t in range(dst // T, (dst + length - 1) // T + 1):
                for u in range(src // T, (src + length - 1) // T + 1):
                    low = max(dst, t * T, dst + T * u - src) - t * T
                    high = min(dst + length, (t + 1) * T, dst + T * (u + 1) - src) - t * T
                    if low >= high:
                        continue
                    tile = ATT[block_rows, u * T : (u + 1) * T].astype(F32)
                    shift = (dst - src) % T
                    if shift:
                        tile = pltpu.roll(tile, shift, 1)
                    if t in done:
                        tile = jnp.where((lane >= low) & (lane < high), tile, done[t])
                    done[t] = tile
        for t, tile in done.items():
            ATR[block_rows, t * T : (t + 1) * T] = tile.astype(BF)
        return carry

    def place(n):
        return (4 + ((n + 1) // 2) * (2 * (n % 2) - 1)) % 8

    def gy_copy(e, way):
        return remote(
            PG.at[zz(e), :, pl.ds(pl.multiple_of(take_col + 256 * way, T), 256)],
            YR.at[e, :, pl.ds(256 * way, 256)],
            gys.at[e, way], gyr.at[e, way], along_y(1 - 2 * way),
        )

    def partial_product(n, carry):
        e = place(n)
        for start, size in ((0, 512), (512, 640), (1152, 512)):
            prod = dot(OGR[zz(e), :, 0:RP], ATR[:, start : start + size], 0, 0)
            PG[zz(e), :, start : start + size] = prod.astype(BF)
        for way in (0, 1):
            gy_copy(e, way).start()
        return carry

    def gx_copy(e, half):
        turn = (half + min(e, 8 - e)) % 2
        return remote(
            PG.at[zz(e), rows(half), pl.ds(own_col, CARRY)],
            XR.at[e, rows(half), :],
            gxs.at[e, half], gxr.at[e, half], along_x(1 - 2 * turn),
        )

    def add_y(low):
        e = place(low)
        for way in (0, 1):
            gy_copy(e, way).wait_recv()
        cols = pl.ds(give_col, SHARE)
        PG[zz(e), :, cols] = (PG[zz(e), :, cols].astype(F32) + YR[e].astype(F32)).astype(BF)

        @pl.when(is_b)
        def _():
            if not SPARE_X:
                send = True
            elif low == 0:
                send = False
                for half in (0, 1):
                    gz_copy(half, half, 4).start()
            else:
                send = True
                if low in (1, 2):
                    half = 2 - low
                    gz_copy(half, half, 4).wait_recv()
                    span = rows(half)
                    mid = pl.ds(own_col, CARRY)
                    PG[zz(e), span, mid] = (
                        PG[zz(e), span, mid].astype(F32) + ZR[half, 3, span, :].astype(F32)
                    ).astype(BF)
            if send:
                for half in (0, 1):
                    gx_copy(e, half).start()

    def add_x(n):
        if SPARE_X and n == 0:
            return

        @pl.when(is_a)
        def _():
            e = place(n)
            for half in (0, 1):
                gx_copy(e, half).wait_recv()
            cols = pl.ds(own_col, CARRY)
            PG[zz(e), :, cols] = (PG[zz(e), :, cols].astype(F32) + XR[e].astype(F32)).astype(BF)

    def gz_copy(way, half, reach):
        e = reach if way == 0 else 8 - reach
        return remote(
            PG.at[zz(e), rows(half), pl.ds(own_col, CARRY)],
            ZR.at[way, reach - 1, rows(half), :],
            gzs.at[way, half, reach - 1], gzr.at[way, half, reach - 1], along_z(1 - 2 * way),
        )

    def serve_gz(reach, halves=(0, 1)):
        @pl.when(is_a)
        def _():
            for half in halves:
                for way in (0, 1):
                    top = chain(way, half)
                    if reach > top:
                        continue
                    if reach < top:
                        gz_copy(way, half, reach + 1).wait_recv()
                        e = (reach if way == 0 else 8 - reach) % 8
                        span = rows(half)
                        cols = pl.ds(own_col, CARRY)
                        PG[zz(e), span, cols] = (
                            PG[zz(e), span, cols].astype(F32) + ZR[way, reach, span, :].astype(F32)
                        ).astype(BF)
                    if reach > 0:
                        gz_copy(way, half, reach).start()

    turns = [(dy, dx) for dy in range(4) for dx in range(2)][1:]

    def owner(dy, dx):
        return (((y + dy) % 4) * 2 + (xh if dx == 0 else 1 - xh))

    def f_copy(dy, dx, half):
        slot = 2 * dy + dx
        size = 256 if dy % 2 == 0 else T
        return remote(
            LB.at[owner(dy, dx), rows(half), pl.ds(0, size)],
            FR.at[slot, rows(half), pl.ds(0, size)],
            fs.at[slot, half], fr.at[slot, half], owner_device(dy, dx),
        )

    def send_last(half):
        span = rows(half)
        for j in range(8):
            u, shift = divmod(80 * j, T)
            tile = PG[z, span, SHARE + u * T : SHARE + (u + 1) * T].astype(F32)
            if shift:
                tile = pltpu.roll(tile, T - shift, 1)
            if shift + 80 > T:
                more = PG[z, span, SHARE + (u + 1) * T : SHARE + (u + 2) * T].astype(F32)
                tile = jnp.where(lanes(SPAN[half][1]) < T - shift, tile, pltpu.roll(more, T - shift, 1))
            LB[j, span, 0:T] = tile.astype(BF)
        for m in range(4):
            j = (m // 2) * 4 + m % 2 + 2 * par
            LB[j, span, T : 2 * T] = PG[z, span, pl.ds(pl.multiple_of(par * CARRY + m * T, T), T)]
        for dy, dx in turns:
            f_copy(dy, dx, half).start()

    share = remote(SS, SR, cs.at[2], cr.at[2], sibling)

    def finish():
        me = owner(0, 0)
        rest = LB[me, :, 0:T].astype(F32)
        main = LB[me, :, T : 2 * T].astype(F32)
        for dy, dx in turns:
            for half in (0, 1):
                f_copy(dy, dx, half).wait_recv()
            rest = rest + FR[2 * dy + dx, :, 0:T].astype(F32)
            if dy % 2 == 0:
                main = main + FR[2 * dy + dx, :, T : 2 * T].astype(F32)
        norm = 1.0 / math.sqrt(TOK * 256)
        main = main * norm
        rest = rest * norm
        second = jnp.where(lanes(RP) < 24, pltpu.roll(main, 24, 1), pltpu.roll(rest, 24, 1))
        SS[...] = jnp.where(c == 0, second, main)
        share.start()
        wg_ref[...] = jnp.where(c == 0, main, second)[0:RB, 0:104]

    def block(who, e):
        return mine(e) if who == 0 else theirs(e)

    def grad_in(who, group):
        for start, size in ((0, 512), (512, 640), (1152, 512)):
            cols = pl.ds(start, size)
            prods = [
                dot(OGR[zz(e), 0:TOK, 0:RP] if who == 0 else OGS[zz(e), :, 0:RP], W[block(who, e), :, cols], 1, 0)
                for e in group
            ]
            AGF[:, cols] += sum(prods[1:], prods[0])

    def project(who, group):
        att = ATT[...]
        lane = lanes(TOK)
        done = []
        for e in group:
            prod = dot(att, W[block(who, e)], 1, 1)
            shift = (RB * block(who, e)) % T
            one = pltpu.roll(prod[:, 0:T], shift, 1)
            tail = jnp.concatenate([prod[:, T:RP], jnp.zeros((TOK, 2 * T - RP), F32)], axis=1)
            two = pltpu.roll(tail, shift, 1)
            done.append((shift, one, two))
        for e, (shift, one, two) in zip(group, done):
            first = (RB * block(who, e)) // T

            def put(n, mask, value):
                cols = pl.ds(pl.multiple_of(jnp.minimum(first + n, D // T - 1) * T, T), T)
                old = LO[:, cols]
                new = (old.astype(F32) + value).astype(BF)
                LO[:, cols] = jnp.where(mask, new, old)

            put(0, lane >= shift, one)
            put(1, lane - shift < RB - T, jnp.where(lane < shift, one, two))
            put(2, lane < shift - (2 * T - RB), two)

    def backward(low, high):
        cols = [head_columns(h) for h in range(low, high)]
        qs, ks, vs, douts, atts = [[ref[:, col] for col in cols] for ref in (Q, K, V, AGB, ATT)]
        probs = [PST[h] for h in range(low, high)]
        deltas = [
            jnp.sum(dout.astype(F32) * att.astype(F32), axis=1, keepdims=True) for dout, att in zip(douts, atts)
        ]
        prob_grads = [dot(dout, v, 1, 1) for dout, v in zip(douts, vs)]
        grads = [(p * (g - delta)).astype(BF) for p, g, delta in zip(probs, prob_grads, deltas)]
        dvs = [dot(p.astype(BF), dout, 0, 0).astype(BF) for p, dout in zip(probs, douts)]
        dqs = [(dot(g, k, 1, 0) * factor).astype(BF) for g, k in zip(grads, ks)]
        dks = [(dot(g, q, 0, 0) * factor).astype(BF) for g, q in zip(grads, qs)]
        for n, col in enumerate(cols):
            Q[:, col] = dqs[n]
            K[:, col] = dks[n]
            V[:, col] = dvs[n]

    def loop(low, high, what):
        lax.fori_loop(low, high, what, 0)

    def serve_s(n):
        for e, half in chunks[n]:
            def go(e=e, half=half):
                for kind in (0, 1):
                    s_copy(e, half, kind, theirs).wait_recv()

            if e == 0:
                pl.when(is_a)(go)
            else:
                go()

    def zero_grad():
        AGF[...] = jnp.zeros((TOK, HD), F32)

    def round_grad():
        AGB[...] = AGF[...].astype(BF)

    def shares():
        og_share.wait()
        at_share.wait()

    does = {
        "load": lambda n: loads[n].wait(),
        "og": lambda a, b: loop(a, b, og_blocks),
        "ogs": og_share.start,
        "fwd": forward,
        "ord": lambda: loop(0, 4, order_columns),
        "ats": at_share.start,
        "shares": shares,
        "Z": serve_z, "X": serve_x, "S": serve_s,
        "YA": lambda n: serve_y(n, is_a),
        "YB": lambda n: serve_y(n, is_b),
        "part": lambda a, b: loop(a, b, partial_product),
        "ay": lambda a, b: add_y(a),
        "ax": lambda a, b: add_x(a),
        "gz": serve_gz,
        "zero": zero_grad,
        "E": lambda who, n: grad_in(who, GROUPS[n]),
        "G": lambda who, n: project(who, GROUPS[n]),
        "round": round_grad,
        "bwd": backward,
        "gz0": lambda half: serve_gz(0, (half,)),
        "last": lambda half: pl.when(is_a)(functools.partial(send_last, half)),
        "fin": lambda: pl.when(is_a)(finish),
    }
    for name, *args in PLAN:
        does[name](*args)

    @pl.when(is_b)
    def _():
        share.wait_recv()
        wg_ref[...] = SR[0:RB, 0:104]

    for n in range(8):
        for e, half in chunks[n]:
            def sent(e=e, half=half):
                for way in (0, 1):
                    y_copy(e, half, way).wait_send()
                for kind in (0, 1):
                    s_copy(e, half, kind).wait_send()

            if e == 0:
                pl.when(is_b)(sent)
            else:
                sent()

    def sent_y(e, carry):
        for way in (0, 1):
            gy_copy(e, way).wait_send()
        return carry

    loop(0, 8, sent_y)

    @pl.when(is_b)
    def _():
        for e in range(8):
            if SPARE_X and e == 4:
                continue
            for half in (0, 1):
                gx_copy(e, half).wait_send()
        for half in (0, 1):
            z_copy(half, half, 4).wait_send()
            if SPARE_X:
                gz_copy(half, half, 4).wait_send()

    @pl.when(is_a)
    def _():
        for e in (0, 1, 2, 3, 5, 6, 7):
            for half in (0, 1):
                x_copy(e, half).wait_send()
        for half in (0, 1):
            for way in (0, 1):
                for step in range(1, chain(way, half) + 1):
                    z_copy(way, half, step).wait_send()
                    gz_copy(way, half, step).wait_send()
        for dy, dx in turns:
            for half in (0, 1):
                f_copy(dy, dx, half).wait_send()
        share.wait_send()


def store_kernel(*refs):
    sems = refs[-1]
    copies = [pltpu.make_async_copy(refs[n], refs[5 + n], sems.at[n]) for n in range(5)]
    for copy in copies:
        copy.start()
    for copy in copies:
        copy.wait()


def block_step(residual_in, queries, keys, values, segment_ids, weight_codes, weight_exponents, out_grad):
    vmem = pl.BlockSpec(memory_space=pltpu.VMEM)
    hbm = pl.BlockSpec(memory_space=pl.ANY)
    dma = pltpu.SemaphoreType.DMA
    V = pltpu.VMEM
    shapes = (((TOK, D), BF), ((TOK, HD), BF), ((TOK, HD), BF), ((TOK, HD), BF), ((RB, 104), F32))
    args = (segment_ids, weight_codes, weight_exponents.T, queries, keys, values, out_grad, residual_in)
    args = [pltpu.with_memory_space_constraint(arg, pltpu.HBM) for arg in args]
    outs = pl.pallas_call(
        body_kernel,
        out_shape=tuple(V(*shape) for shape in shapes),
        in_specs=[pl.BlockSpec(memory_space=pltpu.HBM)] * 8,
        out_specs=(vmem,) * 5,
        scratch_shapes=[
            V((16, RP, HD), BF),
            V((8, RP, HD), BF),
            V((8, RP, SHARE), BF),
            V((8, RP, CARRY), BF),
            V((2, 4, RP, CARRY), BF),
            V((8, RP, 2 * T), BF),
            V((8, RP, 2 * T), BF),
            V((RP, T), F32),
            V((RP, T), F32),
            V((8, 2 * TOK, 2 * T), BF),
            V((8, TOK, 2 * T), BF),
            V((2 * TOK, HD), BF),
            V((TOK, HD), BF),
            V((HEADS, TOK, TOK), F32),
            V((TOK, HD), F32),
            V((TOK, HD), BF),
            V((TOK, D), BF),
            V((TOK, TOK), F32),
            V((RB, HD), BF),
            V((HD // BLOCK, RB), jnp.int32),
            V((1, TOK), jnp.int32),
            dma((8,)),
            dma((2, 2, 4)), dma((2, 2, 4)),
            dma((8, 2)), dma((8, 2)),
            dma((8, 2, 2)), dma((8, 2, 2)),
            dma((8, 2, 2)), dma((8, 2, 2)),
            dma((8, 2)), dma((8, 2)),
            dma((8, 2)), dma((8, 2)),
            dma((2, 2, 4)), dma((2, 2, 4)),
            dma((8, 2)), dma((8, 2)),
            dma((3,)), dma((3,)),
        ],
        compiler_params=pltpu.CompilerParams(
            collective_id=0, has_side_effects=True, vmem_limit_bytes=48 * 2**20
        ),
        cost_estimate=pl.CostEstimate(flops=10**10, bytes_accessed=2 * 10**7, transcendentals=10**6),
    )(*args)
    outs = [pltpu.with_memory_space_constraint(out, pltpu.VMEM) for out in outs]
    return pl.pallas_call(
        store_kernel,
        out_shape=tuple(jax.ShapeDtypeStruct(*shape) for shape in shapes),
        in_specs=[hbm] * 5,
        out_specs=(hbm,) * 5,
        scratch_shapes=[dma((5,))],
        compiler_params=pltpu.CompilerParams(vmem_limit_bytes=2**20),
    )(*outs)


def solution(mesh):
    tokens = P(("outer", "inner"), None)
    in_specs = (tokens, tokens, tokens, tokens, tokens, P("inner", None), P("inner", None), tokens)
    out_specs = (tokens, tokens, tokens, tokens, P("inner", "outer"))
    return jax.shard_map(block_step, mesh=mesh, in_specs=in_specs, out_specs=out_specs, check_vma=False)
```

```python
import functools
import math

import jax
import jax.numpy as jnp
from jax import lax
from jax.experimental import pallas as pl
from jax.experimental.pallas import tpu as pltpu
from jax.sharding import PartitionSpec as P

MESH = pl.DeviceIdType.MESH
BF = jnp.bfloat16
F32 = jnp.float32

TOK = 256
D = 3200
HD = 1664
HEADS = 13
BLOCK = 32
T = 128
RB = 200
RP = 208
SPAN = ((0, 112), (112, 96))
CARRY = 1152
SHARE = 512
SPARE_X = True
TOP = (4, 3)

GROUPS = ((0,), (7, 1), (6, 2), (5, 3), (4,))

PLAN = (
    ("load", 6), ("load", 5), ("load", 4), ("load", 3), ("og", 0, 4), ("fwd", 0, 2), ("og", 4, 8), ("fwd", 2, 4),
    ("fwd", 4, 6), ("fwd", 6, 8), ("load", 7), ("fwd", 8, 10), ("ogs",), ("fwd", 10, 12), ("fwd", 12, 13), ("ord",),
    ("ats",), ("Z", 1), ("X", 0), ("Z", 2), ("shares",), ("YB", 0), ("part", 0, 1), ("X", 1), ("part", 1, 2),
    ("Z", 3), ("part", 2, 3), ("Z", 4), ("ay", 0, 1), ("YA", 1), ("part", 3, 4), ("Z", 5), ("part", 4, 5),
    ("ax", 0, 1), ("YA", 2), ("X", 2), ("Z", 6), ("YA", 3), ("part", 5, 6), ("zero",), ("S", 0), ("gz", 4),
    ("ay", 1, 2), ("part", 6, 7), ("ay", 2, 3), ("X", 3), ("E", 0, 0), ("X", 4), ("ax", 1, 2), ("ay", 3, 4),
    ("YB", 1), ("part", 7, 8), ("X", 5), ("YA", 4), ("X", 6), ("ax", 2, 3), ("gz", 3), ("ax", 3, 4), ("ay", 4, 5),
    ("S", 1), ("ax", 4, 5), ("gz", 2), ("ay", 5, 6), ("S", 2), ("ay", 6, 7), ("YB", 2), ("Z", 7), ("G", 1, 0),
    ("YB", 3), ("S", 3), ("ax", 5, 6), ("E", 1, 0), ("ax", 6, 7), ("gz", 1), ("X", 7), ("YB", 4), ("ay", 7, 8),
    ("G", 0, 1), ("YA", 5), ("ax", 7, 8), ("E", 0, 2), ("YB", 5), ("S", 4), ("YA", 6), ("G", 0, 0), ("YB", 6),
    ("gz0", 0), ("YB", 7), ("YA", 7), ("E", 0, 3), ("S", 5), ("last", 0), ("G", 0, 3), ("G", 1, 1), ("E", 0, 4),
    ("gz0", 1), ("S", 6), ("last", 1), ("S", 7), ("E", 1, 3), ("E", 1, 1), ("E", 0, 1), ("E", 1, 2), ("G", 0, 4),
    ("G", 0, 2), ("G", 1, 2), ("E", 1, 4), ("round",), ("bwd", 0, 2), ("bwd", 2, 4), ("bwd", 4, 6), ("G", 1, 4),
    ("bwd", 6, 8), ("fin",), ("G", 1, 3), ("bwd", 8, 10), ("bwd", 10, 12), ("bwd", 12, 13),
)


def chain(way, half):
    return TOP[half] if way == 0 else TOP[1 - half]


def dot(a, b, ca, cb):
    return lax.dot_general(a, b, (((ca,), (cb,)), ((), ())), preferred_element_type=F32)


def lanes(rows):
    return lax.broadcasted_iota(jnp.int32, (rows, T), 1)


def body_kernel(
    seg_hbm, codes_hbm, exps_hbm, q_hbm, k_hbm, v_hbm, og_hbm, res_hbm,
    LO, Q, K, V, wg_ref,
    W, PG, YR, XR, ZR, LB, FR, SR, SS, OGR, OGS, ATR, ATT, PST, AGF, AGB, OG, BIAS, CODES, EXPS, SEG,
    in_sem, zs, zr, xs, xr, ys, yr, ss, sr, gys, gyr, gxs, gxr, gzs, gzr, fs, fr, cs, cr,
):
    o = lax.axis_index("outer")
    i = lax.axis_index("inner")
    y = o // 4
    xh = (o // 2) % 2
    c = o % 2
    xl = i // 8
    z = i % 8
    x = xh * 2 + xl
    par = y % 2
    is_a = c == xl
    is_b = c != xl
    own_col = pl.multiple_of(par * SHARE, T)
    give_col = pl.multiple_of(par * CARRY, T)
    take_col = pl.multiple_of((1 - par) * CARRY, T)

    def device(x_, y_, z_, c_):
        return ((y_ * 2 + x_ // 2) * 2 + c_, (x_ % 2) * 8 + z_)

    def along_x(step):
        return device((x + step + 4) % 4, y, z, c)

    def along_y(step):
        return device(x, (y + step + 4) % 4, z, c)

    def along_z(step):
        return device(x, y, (z + step + 8) % 8, c)

    sibling = device(x, y, z, 1 - c)

    def owner_device(dy, dx):
        return device((xh if dx == 0 else 1 - xh) * 2 + xl, (y + dy) % 4, z, c)

    def remote(src, dst, ssem, rsem, dev):
        return pltpu.make_async_remote_copy(
            src_ref=src, dst_ref=dst, send_sem=ssem, recv_sem=rsem, device_id=dev, device_id_type=MESH
        )

    loads = [
        pltpu.make_async_copy(src, dst, in_sem.at[n])
        for n, (src, dst) in enumerate(
            ((codes_hbm, CODES), (exps_hbm, EXPS), (seg_hbm, SEG), (q_hbm, Q), (k_hbm, K), (v_hbm, V), (og_hbm, OG), (res_hbm, LO))
        )
    ]
    for n in (1, 0, 2):
        loads[n].start()
    barrier = pltpu.get_barrier_semaphore()
    greet = [along_z(1), along_z(-1), along_x(1), along_x(-1), along_y(1), along_y(-1), sibling]
    greet += [owner_device(2, 0), owner_device(0, 1), owner_device(1, 1), owner_device(2, 1), owner_device(3, 1)]
    for dev in greet:
        pl.semaphore_signal(barrier, inc=1, device_id=dev, device_id_type=MESH)

    loads[1].wait()
    exps = EXPS[...]
    scale = jnp.zeros(exps.shape, F32)
    for octave in range(-16, 1):
        scale = scale + jnp.where(exps == octave, 2.0**octave, 0.0)
    spread = (
        lax.broadcasted_iota(jnp.int32, (HD // BLOCK, HD), 1) // BLOCK
        == lax.broadcasted_iota(jnp.int32, (HD // BLOCK, HD), 0)
    ).astype(BF)
    wide = dot(scale.astype(BF), spread, 0, 0)
    loads[0].wait()
    for load in loads[3:]:
        load.start()
    loads[2].wait()
    block = CODES[...].astype(F32) * wide
    block = jnp.concatenate([block, jnp.zeros((RP - RB, HD), F32)], axis=0)
    W[xl * 8 + z] = block.astype(BF)

    pl.semaphore_wait(barrier, len(greet))

    def zz(e):
        return (z + e) % 8

    def rows(half):
        return pl.ds(*SPAN[half])

    def mine(e):
        return c * 8 + zz(e)

    def theirs(e):
        return (1 - c) * 8 + zz(e)

    def z_copy(way, half, step):
        e = (9 - step) % 8 if way == 0 else step - 1
        part = W.at[mine(e), rows(half), pl.ds(own_col, CARRY)]
        return remote(part, part, zs.at[way, half, step - 1], zr.at[way, half, step - 1], along_z(1 - 2 * way))

    def z_arrival(way, half, step):
        e = 8 - step if way == 0 else step
        part = W.at[mine(e), rows(half), pl.ds(own_col, CARRY)]
        return remote(part, part, zs.at[way, half, step - 1], zr.at[way, half, step - 1], along_z(1 - 2 * way))

    def x_copy(e, half):
        part = W.at[mine(e), rows(half), pl.ds(own_col, CARRY)]
        turn = (half + (e > 4)) % 2
        return remote(part, part, xs.at[e, half], xr.at[e, half], along_x(1 - 2 * turn))

    def y_copy(e, half, way):
        part = W.at[mine(e), rows(half), pl.ds(pl.multiple_of(give_col + 256 * way, T), 256)]
        return remote(part, part, ys.at[e, half, way], yr.at[e, half, way], along_y(1 - 2 * way))

    def y_arrival(e, half, way):
        part = W.at[mine(e), rows(half), pl.ds(pl.multiple_of(take_col + 256 * way, T), 256)]
        return remote(part, part, ys.at[e, half, way], yr.at[e, half, way], along_y(1 - 2 * way))

    def s_copy(e, half, kind, at=mine):
        cols = pl.ds(own_col, CARRY) if kind == 0 else pl.ds(take_col, SHARE)
        part = W.at[at(e), rows(half), cols]
        return remote(part, part, ss.at[e, half, kind], sr.at[e, half, kind], sibling)

    def spread_out(e, half):
        for way in (0, 1):
            y_copy(e, half, way).start()
        s_copy(e, half, 0).start()

    chunks = [
        [(0, 0), (0, 1)],
        [(7, 0), (1, 0)], [(7, 1), (1, 1)], [(6, 0), (2, 0)], [(6, 1), (2, 1)],
        [(5, 0), (3, 0)], [(5, 1), (3, 1)], [(4, 0), (4, 1)],
    ]

    def serve_z(n):
        @pl.when(is_a)
        def _():
            for e, half in chunks[n]:
                way = (0 if half == 0 else 1) if e == 4 else (0 if e > 4 else 1)
                step = 8 - e if way == 0 else e
                z_arrival(way, half, step).wait_recv()
                if step < chain(way, half):
                    z_copy(way, half, step + 1).start()
                if e != 4:
                    x_copy(e, half).start()
                spread_out(e, half)

    def serve_x(n):
        @pl.when(is_b)
        def _():
            for e, half in chunks[n]:
                if e == 4:
                    z_arrival(half, half, 4).wait_recv()
                else:
                    x_copy(e, half).wait_recv()
                if (e, half) in ((5, 0), (3, 1)):
                    z_copy(half, half, 4).start()
                spread_out(e, half)

    def serve_y(n, role):
        @pl.when(role)
        def _():
            for e, half in chunks[n]:
                for way in (0, 1):
                    y_arrival(e, half, way).wait_recv()
                s_copy(e, half, 1).start()

    @pl.when(is_a)
    def _():
        for half in (0, 1):
            for way in (0, 1):
                z_copy(way, half, 1).start()
            x_copy(0, half).start()

    seg = jnp.broadcast_to(SEG[...].astype(F32), (TOK, TOK))
    BIAS[...] = jnp.where(seg == seg.T, 0.0, -1e30)
    factor = 1.0 / math.sqrt(T)

    def head_columns(h):
        return slice(h * T, (h + 1) * T)

    def forward(low, high):
        cols = [head_columns(h) for h in range(low, high)]
        qs, ks, vs = [[ref[:, col] for col in cols] for ref in (Q, K, V)]
        bias = BIAS[...]
        scores = [dot(q, k, 1, 1) * factor + bias for q, k in zip(qs, ks)]
        tops = [jnp.max(s, axis=1, keepdims=True) for s in scores]
        scores = [jnp.exp(s - top) for s, top in zip(scores, tops)]
        sums = [1.0 / jnp.sum(s, axis=1, keepdims=True) for s in scores]
        probs = [s * inverse for s, inverse in zip(scores, sums)]
        outs = [dot(p.astype(BF), v, 1, 0).astype(BF) for p, v in zip(probs, vs)]
        for n, h in enumerate(range(low, high)):
            PST[h] = probs[n]
            ATT[:, cols[n]] = outs[n]

    def og_blocks(kz, carry):
        lane = lanes(TOK)
        for other in (0, 1):
            b = (c if other == 0 else 1 - c) * 8 + kz
            first = (RB * b) // T
            shift = (RB * b) % T
            back = (T - shift) % T
            tiles = [
                pltpu.roll(
                    OG[:, pl.ds(pl.multiple_of(jnp.minimum(first + n, D // T - 1) * T, T), T)].astype(F32), back, 1
                )
                for n in range(3)
            ]
            left = jnp.where(lane < T - shift, tiles[0], tiles[1]).astype(BF)
            right = jnp.where(lane < T - shift, tiles[1], tiles[2])
            right = jnp.where(lane < RB - T, right, 0.0).astype(BF)
            if other == 0:
                OGR[kz, 0:TOK, 0:T] = left
                OGR[kz, 0:TOK, T : 2 * T] = right
            else:
                OGS[kz, :, 0:T] = left
                OGS[kz, :, T : 2 * T] = right
        return carry

    og_share = remote(OGS, OGR.at[:, pl.ds(TOK, TOK), :], cs.at[0], cr.at[0], sibling)
    at_share = remote(ATR.at[pl.ds(0, TOK), :], ATR.at[pl.ds(TOK, TOK), :], cs.at[1], cr.at[1], sibling)

    pieces = []
    for j in range(8):
        pos = (j // 2 % 2) * 9 + (j // 4) * 2 + j % 2
        pieces.append((pos * T, 208 * j, T))
        pieces.append((SHARE + 80 * j, 208 * j + T, 80))

    def order_columns(n, carry):
        size = 64
        block_rows = pl.ds(pl.multiple_of(n * size, size), size)
        lane = lanes(size)
        done = {}
        for dst, src, length in pieces:
            for t in range(dst // T, (dst + length - 1) // T + 1):
                for u in range(src // T, (src + length - 1) // T + 1):
                    low = max(dst, t * T, dst + T * u - src) - t * T
                    high = min(dst + length, (t + 1) * T, dst + T * (u + 1) - src) - t * T
                    if low >= high:
                        continue
                    tile = ATT[block_rows, u * T : (u + 1) * T].astype(F32)
                    shift = (dst - src) % T
                    if shift:
                        tile = pltpu.roll(tile, shift, 1)
                    if t in done:
                        tile = jnp.where((lane >= low) & (lane < high), tile, done[t])
                    done[t] = tile
        for t, tile in done.items():
            ATR[block_rows, t * T : (t + 1) * T] = tile.astype(BF)
        return carry

    def place(n):
        return (4 + ((n + 1) // 2) * (2 * (n % 2) - 1)) % 8

    def gy_copy(e, way):
        return remote(
            PG.at[zz(e), :, pl.ds(pl.multiple_of(take_col + 256 * way, T), 256)],
            YR.at[e, :, pl.ds(256 * way, 256)],
            gys.at[e, way], gyr.at[e, way], along_y(1 - 2 * way),
        )

    def partial_product(n, carry):
        e = place(n)
        for start, size in ((0, 512), (512, 640), (1152, 512)):
            prod = dot(OGR[zz(e), :, 0:RP], ATR[:, start : start + size], 0, 0)
            PG[zz(e), :, start : start + size] = prod.astype(BF)
        for way in (0, 1):
            gy_copy(e, way).start()
        return carry

    def gx_copy(e, half):
        turn = (half + min(e, 8 - e)) % 2
        return remote(
            PG.at[zz(e), rows(half), pl.ds(own_col, CARRY)],
            XR.at[e, rows(half), :],
            gxs.at[e, half], gxr.at[e, half], along_x(1 - 2 * turn),
        )

    def add_y(low):
        e = place(low)
        for way in (0, 1):
            gy_copy(e, way).wait_recv()
        cols = pl.ds(give_col, SHARE)
        PG[zz(e), :, cols] = (PG[zz(e), :, cols].astype(F32) + YR[e].astype(F32)).astype(BF)

        @pl.when(is_b)
        def _():
            if not SPARE_X:
                send = True
            elif low == 0:
                send = False
                for half in (0, 1):
                    gz_copy(half, half, 4).start()
            else:
                send = True
                if low in (1, 2):
                    half = 2 - low
                    gz_copy(half, half, 4).wait_recv()
                    span = rows(half)
                    mid = pl.ds(own_col, CARRY)
                    PG[zz(e), span, mid] = (
                        PG[zz(e), span, mid].astype(F32) + ZR[half, 3, span, :].astype(F32)
                    ).astype(BF)
            if send:
                for half in (0, 1):
                    gx_copy(e, half).start()

    def add_x(n):
        if SPARE_X and n == 0:
            return

        @pl.when(is_a)
        def _():
            e = place(n)
            for half in (0, 1):
                gx_copy(e, half).wait_recv()
            cols = pl.ds(own_col, CARRY)
            PG[zz(e), :, cols] = (PG[zz(e), :, cols].astype(F32) + XR[e].astype(F32)).astype(BF)

    def gz_copy(way, half, reach):
        e = reach if way == 0 else 8 - reach
        return remote(
            PG.at[zz(e), rows(half), pl.ds(own_col, CARRY)],
            ZR.at[way, reach - 1, rows(half), :],
            gzs.at[way, half, reach - 1], gzr.at[way, half, reach - 1], along_z(1 - 2 * way),
        )

    def serve_gz(reach, halves=(0, 1)):
        @pl.when(is_a)
        def _():
            for half in halves:
                for way in (0, 1):
                    top = chain(way, half)
                    if reach > top:
                        continue
                    if reach < top:
                        gz_copy(way, half, reach + 1).wait_recv()
                        e = (reach if way == 0 else 8 - reach) % 8
                        span = rows(half)
                        cols = pl.ds(own_col, CARRY)
                        PG[zz(e), span, cols] = (
                            PG[zz(e), span, cols].astype(F32) + ZR[way, reach, span, :].astype(F32)
                        ).astype(BF)
                    if reach > 0:
                        gz_copy(way, half, reach).start()

    turns = [(dy, dx) for dy in range(4) for dx in range(2)][1:]

    def owner(dy, dx):
        return (((y + dy) % 4) * 2 + (xh if dx == 0 else 1 - xh))

    def f_copy(dy, dx, half):
        slot = 2 * dy + dx
        size = 256 if dy % 2 == 0 else T
        return remote(
            LB.at[owner(dy, dx), rows(half), pl.ds(0, size)],
            FR.at[slot, rows(half), pl.ds(0, size)],
            fs.at[slot, half], fr.at[slot, half], owner_device(dy, dx),
        )

    def send_last(half):
        span = rows(half)
        for j in range(8):
            u, shift = divmod(80 * j, T)
            tile = PG[z, span, SHARE + u * T : SHARE + (u + 1) * T].astype(F32)
            if shift:
                tile = pltpu.roll(tile, T - shift, 1)
            if shift + 80 > T:
                more = PG[z, span, SHARE + (u + 1) * T : SHARE + (u + 2) * T].astype(F32)
                tile = jnp.where(lanes(SPAN[half][1]) < T - shift, tile, pltpu.roll(more, T - shift, 1))
            LB[j, span, 0:T] = tile.astype(BF)
        for m in range(4):
            j = (m // 2) * 4 + m % 2 + 2 * par
            LB[j, span, T : 2 * T] = PG[z, span, pl.ds(pl.multiple_of(par * CARRY + m * T, T), T)]
        for dy, dx in turns:
            f_copy(dy, dx, half).start()

    share = remote(SS, SR, cs.at[2], cr.at[2], sibling)

    def finish():
        me = owner(0, 0)
        rest = LB[me, :, 0:T].astype(F32)
        main = LB[me, :, T : 2 * T].astype(F32)
        for dy, dx in turns:
            for half in (0, 1):
                f_copy(dy, dx, half).wait_recv()
            rest = rest + FR[2 * dy + dx, :, 0:T].astype(F32)
            if dy % 2 == 0:
                main = main + FR[2 * dy + dx, :, T : 2 * T].astype(F32)
        norm = 1.0 / math.sqrt(TOK * 256)
        main = main * norm
        rest = rest * norm
        second = jnp.where(lanes(RP) < 24, pltpu.roll(main, 24, 1), pltpu.roll(rest, 24, 1))
        SS[...] = jnp.where(c == 0, second, main)
        share.start()
        wg_ref[...] = jnp.where(c == 0, main, second)[0:RB, 0:104]

    def block(who, e):
        return mine(e) if who == 0 else theirs(e)

    def grad_in(who, group):
        for start, size in ((0, 512), (512, 640), (1152, 512)):
            cols = pl.ds(start, size)
            prods = [
                dot(OGR[zz(e), 0:TOK, 0:RP] if who == 0 else OGS[zz(e), :, 0:RP], W[block(who, e), :, cols], 1, 0)
                for e in group
            ]
            AGF[:, cols] += sum(prods[1:], prods[0])

    def project(who, group):
        att = ATT[...]
        lane = lanes(TOK)
        done = []
        for e in group:
            prod = dot(att, W[block(who, e)], 1, 1)
            shift = (RB * block(who, e)) % T
            one = pltpu.roll(prod[:, 0:T], shift, 1)
            tail = jnp.concatenate([prod[:, T:RP], jnp.zeros((TOK, 2 * T - RP), F32)], axis=1)
            two = pltpu.roll(tail, shift, 1)
            done.append((shift, one, two))
        for e, (shift, one, two) in zip(group, done):
            first = (RB * block(who, e)) // T

            def put(n, mask, value):
                cols = pl.ds(pl.multiple_of(jnp.minimum(first + n, D // T - 1) * T, T), T)
                old = LO[:, cols]
                new = (old.astype(F32) + value).astype(BF)
                LO[:, cols] = jnp.where(mask, new, old)

            put(0, lane >= shift, one)
            put(1, lane - shift < RB - T, jnp.where(lane < shift, one, two))
            put(2, lane < shift - (2 * T - RB), two)

    def backward(low, high):
        cols = [head_columns(h) for h in range(low, high)]
        qs, ks, vs, douts, atts = [[ref[:, col] for col in cols] for ref in (Q, K, V, AGB, ATT)]
        probs = [PST[h] for h in range(low, high)]
        deltas = [
            jnp.sum(dout.astype(F32) * att.astype(F32), axis=1, keepdims=True) for dout, att in zip(douts, atts)
        ]
        prob_grads = [dot(dout, v, 1, 1) for dout, v in zip(douts, vs)]
        grads = [(p * (g - delta)).astype(BF) for p, g, delta in zip(probs, prob_grads, deltas)]
        dvs = [dot(p.astype(BF), dout, 0, 0).astype(BF) for p, dout in zip(probs, douts)]
        dqs = [(dot(g, k, 1, 0) * factor).astype(BF) for g, k in zip(grads, ks)]
        dks = [(dot(g, q, 0, 0) * factor).astype(BF) for g, q in zip(grads, qs)]
        for n, col in enumerate(cols):
            Q[:, col] = dqs[n]
            K[:, col] = dks[n]
            V[:, col] = dvs[n]

    def loop(low, high, what):
        lax.fori_loop(low, high, what, 0)

    def serve_s(n):
        for e, half in chunks[n]:
            def go(e=e, half=half):
                for kind in (0, 1):
                    s_copy(e, half, kind, theirs).wait_recv()

            if e == 0:
                pl.when(is_a)(go)
            else:
                go()

    def zero_grad():
        AGF[...] = jnp.zeros((TOK, HD), F32)

    def round_grad():
        AGB[...] = AGF[...].astype(BF)

    def shares():
        og_share.wait()
        at_share.wait()

    does = {
        "load": lambda n: loads[n].wait(),
        "og": lambda a, b: loop(a, b, og_blocks),
        "ogs": og_share.start,
        "fwd": forward,
        "ord": lambda: loop(0, 4, order_columns),
        "ats": at_share.start,
        "shares": shares,
        "Z": serve_z, "X": serve_x, "S": serve_s,
        "YA": lambda n: serve_y(n, is_a),
        "YB": lambda n: serve_y(n, is_b),
        "part": lambda a, b: loop(a, b, partial_product),
        "ay": lambda a, b: add_y(a),
        "ax": lambda a, b: add_x(a),
        "gz": serve_gz,
        "zero": zero_grad,
        "E": lambda who, n: grad_in(who, GROUPS[n]),
        "G": lambda who, n: project(who, GROUPS[n]),
        "round": round_grad,
        "bwd": backward,
        "gz0": lambda half: serve_gz(0, (half,)),
        "last": lambda half: pl.when(is_a)(functools.partial(send_last, half)),
        "fin": lambda: pl.when(is_a)(finish),
    }
    for name, *args in PLAN:
        does[name](*args)

    @pl.when(is_b)
    def _():
        share.wait_recv()
        wg_ref[...] = SR[0:RB, 0:104]

    for n in range(8):
        for e, half in chunks[n]:
            def sent(e=e, half=half):
                for way in (0, 1):
                    y_copy(e, half, way).wait_send()
                for kind in (0, 1):
                    s_copy(e, half, kind).wait_send()

            if e == 0:
                pl.when(is_b)(sent)
            else:
                sent()

    def sent_y(e, carry):
        for way in (0, 1):
            gy_copy(e, way).wait_send()
        return carry

    loop(0, 8, sent_y)

    @pl.when(is_b)
    def _():
        for e in range(8):
            if SPARE_X and e == 4:
                continue
            for half in (0, 1):
                gx_copy(e, half).wait_send()
        for half in (0, 1):
            z_copy(half, half, 4).wait_send()
            if SPARE_X:
                gz_copy(half, half, 4).wait_send()

    @pl.when(is_a)
    def _():
        for e in (0, 1, 2, 3, 5, 6, 7):
            for half in (0, 1):
                x_copy(e, half).wait_send()
        for half in (0, 1):
            for way in (0, 1):
                for step in range(1, chain(way, half) + 1):
                    z_copy(way, half, step).wait_send()
                    gz_copy(way, half, step).wait_send()
        for dy, dx in turns:
            for half in (0, 1):
                f_copy(dy, dx, half).wait_send()
        share.wait_send()


def store_kernel(*refs):
    sems = refs[-1]
    copies = [pltpu.make_async_copy(refs[n], refs[5 + n], sems.at[n]) for n in range(5)]
    for copy in copies:
        copy.start()
    for copy in copies:
        copy.wait()


def block_step(residual_in, queries, keys, values, segment_ids, weight_codes, weight_exponents, out_grad):
    vmem = pl.BlockSpec(memory_space=pltpu.VMEM)
    hbm = pl.BlockSpec(memory_space=pl.ANY)
    dma = pltpu.SemaphoreType.DMA
    V = pltpu.VMEM
    shapes = (((TOK, D), BF), ((TOK, HD), BF), ((TOK, HD), BF), ((TOK, HD), BF), ((RB, 104), F32))
    args = (segment_ids, weight_codes, weight_exponents.T, queries, keys, values, out_grad, residual_in)
    args = [pltpu.with_memory_space_constraint(arg, pltpu.HBM) for arg in args]
    outs = pl.pallas_call(
        body_kernel,
        out_shape=tuple(V(*shape) for shape in shapes),
        in_specs=[pl.BlockSpec(memory_space=pltpu.HBM)] * 8,
        out_specs=(vmem,) * 5,
        scratch_shapes=[
            V((16, RP, HD), BF),
            V((8, RP, HD), BF),
            V((8, RP, SHARE), BF),
            V((8, RP, CARRY), BF),
            V((2, 4, RP, CARRY), BF),
            V((8, RP, 2 * T), BF),
            V((8, RP, 2 * T), BF),
            V((RP, T), F32),
            V((RP, T), F32),
            V((8, 2 * TOK, 2 * T), BF),
            V((8, TOK, 2 * T), BF),
            V((2 * TOK, HD), BF),
            V((TOK, HD), BF),
            V((HEADS, TOK, TOK), F32),
            V((TOK, HD), F32),
            V((TOK, HD), BF),
            V((TOK, D), BF),
            V((TOK, TOK), F32),
            V((RB, HD), BF),
            V((HD // BLOCK, RB), jnp.int32),
            V((1, TOK), jnp.int32),
            dma((8,)),
            dma((2, 2, 4)), dma((2, 2, 4)),
            dma((8, 2)), dma((8, 2)),
            dma((8, 2, 2)), dma((8, 2, 2)),
            dma((8, 2, 2)), dma((8, 2, 2)),
            dma((8, 2)), dma((8, 2)),
            dma((8, 2)), dma((8, 2)),
            dma((2, 2, 4)), dma((2, 2, 4)),
            dma((8, 2)), dma((8, 2)),
            dma((3,)), dma((3,)),
        ],
        compiler_params=pltpu.CompilerParams(
            collective_id=0, has_side_effects=True, vmem_limit_bytes=48 * 2**20
        ),
        cost_estimate=pl.CostEstimate(flops=10**10, bytes_accessed=2 * 10**7, transcendentals=10**6),
    )(*args)
    outs = [pltpu.with_memory_space_constraint(out, pltpu.VMEM) for out in outs]
    return pl.pallas_call(
        store_kernel,
        out_shape=tuple(jax.ShapeDtypeStruct(*shape) for shape in shapes),
        in_specs=[hbm] * 5,
        out_specs=(hbm,) * 5,
        scratch_shapes=[dma((5,))],
        compiler_params=pltpu.CompilerParams(vmem_limit_bytes=2**20),
    )(*outs)


def solution(mesh):
    tokens = P(("outer", "inner"), None)
    in_specs = (tokens, tokens, tokens, tokens, tokens, P("inner", None), P("inner", None), tokens)
    out_specs = (tokens, tokens, tokens, tokens, P("inner", "outer"))
    return jax.shard_map(block_step, mesh=mesh, in_specs=in_specs, out_specs=out_specs, check_vma=False)
```
